256 devices in a mesh: ctx: 64 (over x, z, y_hi), uly: 4 (over y_lo, core).
Axes of the slice: x: 4, y: 4 (y_hi: 2, y_lo: 2; y = y_hi * 2 + y_lo), z: 8, core: 2. Of those that a mesh axis runs over, the one named last changes fastest.
Arguments:
- query_rows: bfloat16 [32768, 2560], P(('ctx', 'uly')), may hold values from -8 to 8
- key_rows: bfloat16 [32768, 2560], P(('ctx', 'uly')), may hold values from -8 to 8
- value_rows: bfloat16 [32768, 2560], P(('ctx', 'uly')), may hold values from -6 to 6
- query_tan: bfloat16 [32768, 2560], P(('ctx', 'uly')), may hold values from -6 to 6
- key_tan: bfloat16 [32768, 2560], P(('ctx', 'uly')), may hold values from -6 to 6
- value_tan: bfloat16 [32768, 2560], P(('ctx', 'uly')), may hold values from -6 to 6
- tile_query: int32 [64, 64], P('ctx'), may hold values from 0 to 3, as said below
- tile_key: int32 [64, 64], P('ctx'), may hold values from 0 to 15, as said below
- tile_count: int32 [64], P('ctx'), may hold values from 8 to 64
Outputs:
- attended: bfloat16 [32768, 2560], P(('ctx', 'uly'))
- attended_tan: bfloat16 [32768, 2560], P(('ctx', 'uly'))
The draws below stay inside these ranges and needn't reach their ends.
Inputs may be any that keep to these rules, and one draw needn't show every extreme that they name: `tile_query`: only the first tile_count[b] entries of row b are listed; pairs in a row are distinct. `tile_key`: A key code c names tile c % 4 of the block c // 4 places before the query's block, going round the loop of 64 blocks.
All inputs are finite; a program needn't handle non-finite values.
Results may differ from the reference program's by a relative error of at most 0.012.
The reference program's roundings to bfloat16 on the way (of `weights_low` and `product_low`) count: a program that leaves them out, or rounds other values in their place, can miss the bound.
Values may be sent and summed in bfloat16 or wider, within the bound.
A program may use at most 128 MiB of HBM per device.

```python
import math
import jax
import jax.numpy as jnp
from jax import lax

HEAD = 128
HEADS = 20
TILE = 128
REACH = 4
MAXT = 64
CT = 512
QT = 4
BLOCKS = 64
TOKENS = 32768
FEAT = 2560


def aligned_pair(key, applied):
    base_query = jnp.clip(jax.random.normal(jax.random.fold_in(key, 101), (TOKENS, FEAT), jnp.float32), -8.0, 8.0)
    base_key = jnp.clip(jax.random.normal(jax.random.fold_in(key, 102), (TOKENS, FEAT), jnp.float32), -8.0, 8.0)
    row_ids = jnp.arange(TOKENS)
    picked = (jax.random.randint(jax.random.fold_in(key, 103), (TOKENS,), 0, 64) == 0) & (row_ids % 2 == 0) & (row_ids % TILE != TILE - 1) & (applied > 0.5)
    strength = 7.5 + 0.5 * jax.random.uniform(jax.random.fold_in(key, 104), (TOKENS,), jnp.float32)
    sign_grid = jnp.where(jax.random.randint(jax.random.fold_in(key, 105), (TOKENS, FEAT), 0, 2) == 0, -1.0, 1.0)
    score_gap = 1.0 + 2.0 * jax.random.uniform(jax.random.fold_in(key, 106), (TOKENS,), jnp.float32)
    lowered = score_gap * math.sqrt(HEAD) / strength
    first_col = (jnp.arange(FEAT) % HEAD == 0)[None, :]
    shared = strength[:, None] * sign_grid
    neighbour = shared - jnp.where(first_col, lowered[:, None] * sign_grid, 0.0)
    next_pick = jnp.concatenate([jnp.zeros((1,), bool), picked[:-1]])
    query_out = jnp.where(picked[:, None], shared, base_query)
    key_out = jnp.where(picked[:, None], shared, jnp.where(next_pick[:, None], jnp.roll(neighbour, 1, axis=0), base_key))
    return (query_out, key_out)


def draw_query_rows(key, part):
    applied = 0.0
    return aligned_pair(key, applied)[0].astype(jnp.bfloat16)


def draw_key_rows(key, part):
    applied = 0.0
    return aligned_pair(key, applied)[1].astype(jnp.bfloat16)


def tile_table(key):
    key_span = REACH * QT
    candidates = QT * key_span
    noise = jax.random.randint(jax.random.fold_in(key, 201), (BLOCKS, candidates), 0, 4096)
    index_row = jnp.arange(candidates)
    behind = index_row % key_span // QT
    favour = (REACH - behind) * 1024
    forced = jnp.where((jnp.arange(BLOCKS)[:, None] == 0) & ((index_row == 0) | (index_row == candidates - 1))[None, :], 16384, 0)
    scores = (noise + favour[None, :] + forced) * candidates + index_row[None, :]
    ranking = jnp.argsort(-scores, axis=1)[:, :MAXT].astype(jnp.int32)
    return (ranking // key_span, ranking % key_span)


def draw_tile_query(key, part):
    return tile_table(key)[0].astype(jnp.int32)


def draw_tile_key(key, part):
    return tile_table(key)[1].astype(jnp.int32)


def draw_tile_count(key, part):
    key = jax.random.fold_in(key, 7)
    subkeys = jax.random.split(key, 3)
    counts = jax.random.randint(subkeys[0], (BLOCKS,), MAXT // 8, MAXT // 2 + 1)
    busiest = jax.random.randint(subkeys[1], (), 0, BLOCKS)
    lightest = (busiest + 1 + jax.random.randint(subkeys[2], (), 0, BLOCKS - 1)) % BLOCKS
    positions = jnp.arange(BLOCKS)
    counts = jnp.where(positions == lightest, MAXT // 8, counts)
    counts = jnp.where(positions == busiest, MAXT, counts)
    return counts.astype(jnp.int32)


def block_levels(rng, extent, cuts, least, high):
    def one(dim, parts):
        steps = jax.random.uniform(jax.random.fold_in(jax.random.fold_in(rng, 6), dim), (parts,), jnp.float32, least / len(cuts), high / len(cuts))
        return jnp.repeat(jnp.exp(steps), extent[dim] // parts).reshape((-1,) + (1,) * (len(extent) - dim - 1))

    gain = one(*cuts[0])
    for cut in cuts[1:]:
        gain = gain * one(*cut)
    return gain


def gaussian(own_key, dims, deviation, bound, cuts=(), held_as=jnp.bfloat16):
    loudness = block_levels(own_key, dims, cuts, -0.22, 0.18) if cuts else 1.0
    array = jax.random.normal(own_key, dims, jnp.float32) * deviation * loudness
    return jnp.minimum(jnp.maximum(array, -bound), bound).astype(held_as)


def setup_inputs(seed: int = 0) -> dict:
    key_of = jax.random.split(jax.random.key(seed), 10)
    return {
        "query_rows": draw_query_rows(jax.random.fold_in(key_of[9], 71), 0),
        "key_rows": draw_key_rows(jax.random.fold_in(key_of[9], 71), 0),
        "value_rows": gaussian(key_of[2], (TOKENS, FEAT), 1.0, 6.0, ((0, 256),)),
        "query_tan": gaussian(key_of[3], (TOKENS, FEAT), 1.0, 6.0, ((0, 256),)),
        "key_tan": gaussian(key_of[4], (TOKENS, FEAT), 1.0, 6.0, ((0, 256),)),
        "value_tan": gaussian(key_of[5], (TOKENS, FEAT), 1.0, 6.0, ((0, 256),)),
        "tile_query": draw_tile_query(jax.random.fold_in(key_of[9], 71), 0),
        "tile_key": draw_tile_key(jax.random.fold_in(key_of[9], 71), 0),
        "tile_count": draw_tile_count(jax.random.fold_in(key_of[9], 71), 0),
    }


def tile_allowed(query_tiles, key_tiles, used_count, tile_rows):
    key_span = REACH * tile_rows
    in_use = jnp.arange(MAXT) < used_count
    pair_code = query_tiles * key_span + key_tiles
    listed = jnp.any((pair_code[:, None] == jnp.arange(tile_rows * key_span)[None, :]) & in_use[:, None], axis=0)
    listed = listed.reshape(tile_rows, key_span)
    own_tile = jnp.arange(key_span)[None, :] == jnp.arange(tile_rows)[:, None]
    return listed | own_tile


def reference(query_rows, key_rows, value_rows, query_tan, key_tan, value_tan, tile_query, tile_key, tile_count):
    scaling = HEAD ** -0.5

    def one_block(inputs):
        block_no, query_tiles, key_tiles, used_count = inputs

        def take_rows(source):
            return lax.dynamic_slice_in_dim(source, (block_no * CT).astype(jnp.int32), CT, 0)

        def band_rows(source):
            pieces = [lax.dynamic_slice_in_dim(source, (((block_no - behind) % BLOCKS) * CT).astype(jnp.int32), CT, 0) for behind in range(REACH)]
            return jnp.concatenate(pieces, 0)

        def split_heads(source):
            return source.reshape(source.shape[0], HEADS, HEAD).astype(jnp.float32)

        allowed = tile_allowed(query_tiles, key_tiles, used_count, QT)
        token_mask = jnp.repeat(jnp.repeat(allowed, TILE, 0), TILE, 1)[None]
        queries = split_heads(take_rows(query_rows))
        tan_queries = split_heads(take_rows(query_tan))
        keys_band = split_heads(band_rows(key_rows))
        values_band = split_heads(band_rows(value_rows))
        tan_keys = split_heads(band_rows(key_tan))
        tan_values = split_heads(band_rows(value_tan))
        scores = scaling * jnp.einsum("qhd,khd->hqk", queries, keys_band)
        score_tan = scaling * (jnp.einsum("qhd,khd->hqk", tan_queries, keys_band) + jnp.einsum("qhd,khd->hqk", queries, tan_keys))
        row_max = jnp.max(jnp.where(token_mask, scores, -1e30), axis=2, keepdims=True)
        weights = jnp.where(token_mask, jnp.exp(scores - row_max), 0.0)
        weight_sum = jnp.sum(weights, axis=2)
        weights_low = lax.optimization_barrier(weights.astype(jnp.bfloat16)).astype(jnp.float32)
        product = weights * score_tan
        linear = jnp.sum(product, axis=2)
        product_low = lax.optimization_barrier(product.astype(jnp.bfloat16)).astype(jnp.float32)
        primal = jnp.einsum("hqk,khd->hqd", weights_low, values_band) / weight_sum[..., None]
        tangent = (jnp.einsum("hqk,khd->hqd", product_low, values_band) + jnp.einsum("hqk,khd->hqd", weights_low, tan_values) - linear[..., None] * primal) / weight_sum[..., None]
        primal_out = jnp.transpose(primal, (1, 0, 2)).reshape(CT, FEAT).astype(jnp.bfloat16)
        tangent_out = jnp.transpose(tangent, (1, 0, 2)).reshape(CT, FEAT).astype(jnp.bfloat16)
        return primal_out, tangent_out

    blocks = jnp.arange(BLOCKS, dtype=jnp.int32)
    primal_all, tangent_all = lax.map(one_block, (blocks, tile_query, tile_key, tile_count))
    return primal_all.reshape(TOKENS, FEAT), tangent_all.reshape(TOKENS, FEAT)
```

```python
import functools
import math
import jax
import jax.numpy as jnp
from jax import lax
from jax.experimental import pallas as pl
from jax.experimental.pallas import tpu as pltpu
from jax.sharding import PartitionSpec as P

HEAD = 128
TILE = 128
REACH = 4
MAXT = 64
LOCAL_HEADS = 5
CT = 512
QT = 4
ROWS = 256
MESH = pl.DeviceIdType.MESH
SCALING = HEAD ** (-0.5)
LOG2E = math.log2(math.e)
NEG = -1e30


def attend(query, keyval, bias, state_max, state_sum, state_lin, acc_w, acc_p, j, slot):
    per = ROWS // TILE
    for i in range(CT // ROWS):
        rows = pl.ds(i * ROWS, ROWS)
        q2 = query[j, rows, :]
        scores = lax.dot_general(
            query[j, rows, HEAD:], keyval[j, slot, 0, :, :HEAD], (((1,), (1,)), ((), ())), preferred_element_type=jnp.float32
        )
        tans = lax.dot_general(
            q2, keyval[j, slot, 0], (((1,), (1,)), ((), ())), preferred_element_type=jnp.float32
        )
        masked = []
        for t in range(per):
            wide = jnp.concatenate([bias[i * per + t, slot, c] for c in range(QT)], axis=1)
            masked.append(jnp.concatenate([wide] * (TILE // 8), axis=0))
        scores = scores * (SCALING * LOG2E) + jnp.concatenate(masked, axis=0)
        old_max = state_max[rows, :]
        new_max = jnp.maximum(old_max, jnp.max(scores, axis=1, keepdims=True))
        alpha = jnp.exp2(old_max - new_max)
        weights = jnp.exp2(scores - new_max[:, :1])
        product = weights * tans
        state_max[rows, :] = new_max
        state_sum[rows, :] = state_sum[rows, :] * alpha + jnp.sum(weights, axis=1, keepdims=True)
        state_lin[rows, :] = state_lin[rows, :] * alpha + jnp.sum(product, axis=1, keepdims=True)
        low = weights.astype(jnp.bfloat16)
        prod_low = product.astype(jnp.bfloat16)
        acc_w[rows, :] = acc_w[rows, :] * alpha[:, :1] + jnp.dot(
            low, keyval[j, slot, 1], preferred_element_type=jnp.float32
        )
        acc_p[rows, :] = acc_p[rows, :] * alpha + jnp.dot(
            prod_low, keyval[j, slot, 1, :, :HEAD], preferred_element_type=jnp.float32
        )


def kernel(
    n_ctx,
    q_ref,
    k_ref,
    v_ref,
    qt_ref,
    kt_ref,
    vt_ref,
    tq_ref,
    tk_ref,
    cnt_ref,
    out_p,
    out_t,
    query,
    keyval,
    bias_own,
    bias,
    st_max,
    st_sum,
    st_lin,
    acc_w,
    acc_p,
    outbuf,
    in_send,
    q_recv,
    kv_recv,
    z1_send,
    z2_send,
    xa_send,
    xb_send,
    bias_send,
    bias_recv,
    out_send,
    out_recv,
):
    ctx = lax.axis_index("ctx")
    uly = lax.axis_index("uly")
    core = lax.rem(uly, 2)
    yh = lax.rem(ctx, 2)
    base = ctx - yh
    y = yh * 2 + lax.div(uly, 2)
    other = uly + 1 - 2 * core
    ahead = lax.rem(ctx + 2, n_ctx)
    behind = lax.rem(ctx + n_ctx - 2, n_ctx)
    at_home = core == yh

    barrier = pltpu.get_barrier_semaphore()
    for step in range(1, 8):
        place = lax.rem(yh * 4 + uly + step, 8)
        pl.semaphore_signal(
            barrier, inc=1, device_id=(base + lax.div(place, 4), lax.rem(place, 4)), device_id_type=MESH
        )
    for where in (ahead, behind):
        for who in (uly, other):
            pl.semaphore_signal(barrier, inc=1, device_id=(where, who), device_id_type=MESH)

    lane = lax.broadcasted_iota(jnp.int32, (8, MAXT), 1)
    codes = jnp.broadcast_to(tk_ref[...], (8, MAXT))
    usable = (lane < cnt_ref[0]) & (jnp.broadcast_to(tq_ref[...], (8, MAXT)) == uly)
    for n in range(REACH):
        for c in range(QT):
            seen = jnp.max(jnp.where(usable & (codes == n * QT + c), 1.0, 0.0), axis=1, keepdims=True)
            if n == 0:
                seen = jnp.maximum(seen, jnp.where(uly == c, 1.0, 0.0))
            bias_own[n, c] = jnp.broadcast_to((1.0 - seen) * NEG, (8, HEAD))

    pl.semaphore_wait(barrier, 11)

    own_rows = pl.ds(pl.multiple_of(uly * TILE, TILE), TILE)
    low_half, high_half = pl.ds(0, HEAD), pl.ds(HEAD, HEAD)

    def group_device(place):
        return (base + lax.div(place, 2), lax.rem(place, 2) * 2 + yh)

    def send_in(j):
        for step in range(4):
            place = lax.rem(y + step, 4)
            cols = pl.ds(pl.multiple_of((place * LOCAL_HEADS + j) * HEAD, HEAD), HEAD)
            moves = (
                (k_ref, keyval.at[j, 0, 0, own_rows, low_half], kv_recv.at[j, 0]),
                (kt_ref, keyval.at[j, 0, 0, own_rows, high_half], kv_recv.at[j, 0]),
                (v_ref, keyval.at[j, 0, 1, own_rows, low_half], kv_recv.at[j, 0]),
                (vt_ref, keyval.at[j, 0, 1, own_rows, high_half], kv_recv.at[j, 0]),
                (q_ref, query.at[j, own_rows, high_half], q_recv.at[j]),
                (qt_ref, query.at[j, own_rows, low_half], q_recv.at[j]),
            )

            def remote():
                for a, (src, dst, sem) in enumerate(moves):
                    pltpu.make_async_remote_copy(
                        src_ref=src.at[:, cols],
                        dst_ref=dst,
                        send_sem=in_send.at[step, a],
                        recv_sem=sem,
                        device_id=group_device(place),
                        device_id_type=MESH,
                    ).start()

            def local():
                for src, dst, sem in moves:
                    pltpu.make_async_copy(src.at[:, cols], dst, sem).start()

            if step == 0:
                pl.when(at_home)(local)
                pl.when(jnp.logical_not(at_home))(remote)
            else:
                remote()

    def bias_copy(step):
        place = lax.rem(y + step, 4)
        return pltpu.make_async_remote_copy(
            src_ref=bias_own,
            dst_ref=bias.at[uly],
            send_sem=bias_send.at[step],
            recv_sem=bias_recv,
            device_id=group_device(place),
            device_id_type=MESH,
        )

    def slot_copy(j, src, dst, sems, ctx_to, uly_to):
        return pltpu.make_async_remote_copy(
            src_ref=keyval.at[j, src],
            dst_ref=keyval.at[j, dst],
            send_sem=sems.at[j],
            recv_sem=kv_recv.at[j, dst],
            device_id=(ctx_to, uly_to),
            device_id_type=MESH,
        )

    def wait_slot(j, slot):
        pltpu.make_async_copy(keyval.at[j, slot], keyval.at[j, slot], kv_recv.at[j, slot]).wait()

    def work(j, slot):
        attend(
            query, keyval, bias, st_max.at[j], st_sum.at[j], st_lin.at[j], acc_w.at[j], acc_p.at[j], j, slot
        )

    def send_out(j):
        cols = pl.ds(pl.multiple_of((y * LOCAL_HEADS + j) * HEAD, HEAD), HEAD)
        for t in range(QT):
            def remote():
                for a, out in enumerate((out_p, out_t)):
                    pltpu.make_async_remote_copy(
                        src_ref=outbuf.at[j, a, pl.ds(t * TILE, TILE), :],
                        dst_ref=out.at[:, cols],
                        send_sem=out_send.at[t, a],
                        recv_sem=out_recv.at[a],
                        device_id=(base + core, t),
                        device_id_type=MESH,
                    ).start()

            def local():
                for a, out in enumerate((out_p, out_t)):
                    pltpu.make_async_copy(
                        outbuf.at[j, a, pl.ds(t * TILE, TILE), :], out.at[:, cols], out_recv.at[a]
                    ).start()

            here = at_home & (uly == t)
            pl.when(here)(local)
            pl.when(jnp.logical_not(here))(remote)

    send_in(0)
    for step in range(4):
        if step == 0:
            @pl.when(at_home)
            def _():
                pltpu.make_async_copy(bias_own, bias.at[uly], bias_recv).start()

            @pl.when(jnp.logical_not(at_home))
            def _():
                bias_copy(0).start()
        else:
            bias_copy(step).start()
    send_in(1)

    @pl.loop(0, LOCAL_HEADS + 2)
    def _(r):
        @pl.when(r < LOCAL_HEADS)
        def _():
            j = r
            wait_slot(j, 0)
            slot_copy(j, 0, 2, z1_send, ahead, uly).start()

            @pl.when(core == 0)
            def _():
                slot_copy(j, 0, 1, xa_send, ctx, other).start()

            @pl.when(j + 2 < LOCAL_HEADS)
            def _():
                send_in(j + 2)

            @pl.when(j == 0)
            def _():
                pltpu.make_async_copy(bias, bias, bias_recv).wait()

            st_max[j] = jnp.full((CT, HEAD), NEG, jnp.float32)
            st_sum[j] = jnp.zeros((CT, HEAD), jnp.float32)
            st_lin[j] = jnp.zeros((CT, HEAD), jnp.float32)
            acc_w[j] = jnp.zeros((CT, 2 * HEAD), jnp.float32)
            acc_p[j] = jnp.zeros((CT, HEAD), jnp.float32)
            pltpu.make_async_copy(query.at[j], query.at[j], q_recv.at[j]).wait()
            work(j, 0)

        @pl.when((r >= 1) & (r < LOCAL_HEADS + 1))
        def _():
            j = r - 1
            wait_slot(j, 2)

            @pl.when(core == 0)
            def _():
                slot_copy(j, 2, 3, xb_send, ctx, other).start()

            @pl.when(core == 1)
            def _():
                slot_copy(j, 2, 3, z2_send, ahead, other).start()
                slot_copy(j, 2, 1, xb_send, ctx, other).start()

            work(j, 2)
            wait_slot(j, 1)
            work(j, 1)

        @pl.when(r >= 2)
        def _():
            j = r - 2
            wait_slot(j, 3)
            work(j, 3)
            inverse = 1.0 / st_sum[j]
            primal = acc_w[j, :, :HEAD] * inverse
            tangent = (
                SCALING * acc_p[j] + acc_w[j, :, HEAD:] - (SCALING * st_lin[j]) * primal
            ) * inverse
            outbuf[j, 0] = primal.astype(jnp.bfloat16)
            outbuf[j, 1] = tangent.astype(jnp.bfloat16)
            send_out(j)

    sources = (k_ref, kt_ref, v_ref, vt_ref, q_ref, qt_ref)
    group = pl.ds(0, LOCAL_HEADS * HEAD)
    for step in range(4):
        def sent():
            for a, src in enumerate(sources):
                pltpu.make_async_copy(src.at[:, group], src.at[:, group], in_send.at[step, a]).wait()
            bias_copy(step).wait_send()

        if step == 0:
            pl.when(jnp.logical_not(at_home))(sent)
        else:
            sent()

    @pl.loop(0, LOCAL_HEADS)
    def _(j):
        slot_copy(j, 0, 2, z1_send, ahead, uly).wait_send()
        slot_copy(j, 2, 3, xb_send, ctx, other).wait_send()

        @pl.when(core == 0)
        def _():
            slot_copy(j, 0, 1, xa_send, ctx, other).wait_send()

        @pl.when(core == 1)
        def _():
            slot_copy(j, 2, 3, z2_send, ahead, other).wait_send()

    for t in range(QT):
        @pl.when(jnp.logical_not(at_home & (uly == t)))
        def _():
            for a, out in enumerate((out_p, out_t)):
                pltpu.make_async_copy(out.at[:, group], out.at[:, group], out_send.at[t, a]).wait()

    pltpu.make_async_copy(out_p, out_p, out_recv.at[0]).wait()
    pltpu.make_async_copy(out_t, out_t, out_recv.at[1]).wait()


def on_device(n_ctx, query_rows, key_rows, value_rows, query_tan, key_tan, value_tan, tile_query, tile_key, tile_count):
    heads = LOCAL_HEADS
    anyspace = pl.BlockSpec(memory_space=pl.ANY)
    vmem = pl.BlockSpec(memory_space=pltpu.VMEM)
    dma = pltpu.SemaphoreType.DMA
    return pl.pallas_call(
        functools.partial(kernel, n_ctx),
        out_shape=(
            jax.ShapeDtypeStruct(query_rows.shape, jnp.bfloat16),
            jax.ShapeDtypeStruct(query_rows.shape, jnp.bfloat16),
        ),
        in_specs=[anyspace] * 6 + [vmem, vmem, pl.BlockSpec(memory_space=pltpu.SMEM)],
        out_specs=(anyspace, anyspace),
        scratch_shapes=[
            pltpu.VMEM((heads, CT, 2 * HEAD), jnp.bfloat16),
            pltpu.VMEM((heads, REACH, 2, CT, 2 * HEAD), jnp.bfloat16),
            pltpu.VMEM((REACH, QT, 8, HEAD), jnp.float32),
            pltpu.VMEM((QT, REACH, QT, 8, HEAD), jnp.float32),
            pltpu.VMEM((heads, CT, HEAD), jnp.float32),
            pltpu.VMEM((heads, CT, HEAD), jnp.float32),
            pltpu.VMEM((heads, CT, HEAD), jnp.float32),
            pltpu.VMEM((heads, CT, 2 * HEAD), jnp.float32),
            pltpu.VMEM((heads, CT, HEAD), jnp.float32),
            pltpu.VMEM((heads, 2, CT, HEAD), jnp.bfloat16),
            dma((4, 6)),
            dma((heads,)),
            dma((heads, REACH)),
            dma((heads,)),
            dma((heads,)),
            dma((heads,)),
            dma((heads,)),
            dma((4,)),
            dma,
            dma((QT, 2)),
            dma((2,)),
        ],
        compiler_params=pltpu.CompilerParams(
            collective_id=0, has_side_effects=True, vmem_limit_bytes=48 * 1024 * 1024
        ),
        cost_estimate=pl.CostEstimate(
            flops=heads * CT * CT * REACH * HEAD * 12,
            bytes_accessed=12 * TILE * 2560,
            transcendentals=heads * CT * CT * REACH,
        ),
        name="band_attention",
    )(query_rows, key_rows, value_rows, query_tan, key_tan, value_tan, tile_query, tile_key, tile_count)


def solution(mesh):
    rows = P(("ctx", "uly"), None)
    return jax.shard_map(
        functools.partial(on_device, mesh.shape["ctx"]),
        mesh=mesh,
        in_specs=(rows,) * 6 + (P("ctx", None), P("ctx", None), P("ctx")),
        out_specs=(rows, rows),
        check_vma=False,
    )
```

```python
import functools
import math
import jax
import jax.numpy as jnp
from jax import lax
from jax.experimental import pallas as pl
from jax.experimental.pallas import tpu as pltpu
from jax.sharding import PartitionSpec as P

HEAD = 128
TILE = 128
REACH = 4
MAXT = 64
LOCAL_HEADS = 5
CT = 512
QT = 4
PART = 256
MESH = pl.DeviceIdType.MESH
SCALING = HEAD ** (-0.5)
LOG2E = math.log2(math.e)
NEG = -1e30


SEND_EVEN = [0, 8, 4, 3, 11, 12, 1, 9, 2, 10]
SEND_ODD = [3, 0, 8, 12, 11, 4, 2, 1, 9, 10]
PLAN_EVEN = [0, 8, 16, 24, 4, 3, 48, 12, 40, 32, 56, 19, 11, 27, 20, 28, 44, 1, 60, 51, 43, 35, 59, 9, 52, 17, 36, 2, 49, 25, 10, 18, 41, 64, 68, 33, 57, 34, 50, 67, 42, 65, 58, 26, 66]
PLAN_ODD = [0, 16, 8, 48, 32, 40, 56, 20, 52, 19, 3, 36, 51, 4, 28, 11, 24, 43, 35, 1, 59, 12, 44, 60, 17, 9, 27, 49, 2, 41, 67, 18, 64, 57, 33, 25, 68, 10, 50, 26, 65, 42, 58, 34, 66]


def look_up(table, at):
    words = [sum(v << (7 * n) for n, v in enumerate(table[w : w + 4])) for w in range(0, len(table), 4)]
    place = at // 4
    word = jnp.int32(words[0])
    for w in range(1, len(words)):
        word = jnp.where(place == w, jnp.int32(words[w]), word)
    return lax.shift_right_logical(word, (at % 4) * 7) % 128


def attend(query, keyval, values_t, bias, j, slot, sink, stats):
    per = PART // TILE
    nt = (((1,), (1,)), ((), ()))
    for h in range(CT // PART):
        cols = pl.ds(h * PART, PART)
        scores = lax.dot_general(
            keyval[j, 0, :, :HEAD], query[j, slot, cols, HEAD:], nt, preferred_element_type=jnp.float32
        )
        tans = lax.dot_general(
            keyval[j, 0], query[j, slot, cols, :], nt, preferred_element_type=jnp.float32
        )
        masked = []
        for c in range(QT):
            wide = jnp.concatenate([bias[slot, h * per + t, c] for t in range(per)], axis=1)
            masked.extend([wide] * (TILE // 8))
        scores = scores * (SCALING * LOG2E) + jnp.concatenate(masked, axis=0)
        top = jnp.max(scores, axis=0, keepdims=True)
        weights = jnp.exp2(scores - top)
        product = weights * tans
        total = jnp.sum(weights, axis=0, keepdims=True)
        inverse = 1.0 / total
        mean_tan = SCALING * jnp.sum(product, axis=0, keepdims=True) * inverse
        by_weight = jnp.dot(values_t[j], weights.astype(jnp.bfloat16), preferred_element_type=jnp.float32)
        by_product = jnp.dot(
            values_t[j, :HEAD, :], product.astype(jnp.bfloat16), preferred_element_type=jnp.float32
        )
        primal = by_weight[:HEAD] * inverse
        tangent = (SCALING * by_product + by_weight[HEAD:]) * inverse - mean_tan * primal
        sink[0, :, cols] = primal.astype(sink.dtype)
        sink[1, :, cols] = tangent.astype(sink.dtype)
        stats[0:1, cols] = top
        stats[1:2, cols] = total
        stats[2:3, cols] = mean_tan


def merge(own, own_stats, came, came_stats, sink):
    for h in range(CT // PART):
        cols = pl.ds(h * PART, PART)
        top_a, top_b = own_stats[0:1, cols], came_stats[0:1, cols]
        tan_a, tan_b = own_stats[2:3, cols], came_stats[2:3, cols]
        top = jnp.maximum(top_a, top_b)
        part_a = own_stats[1:2, cols] * jnp.exp2(top_a - top)
        part_b = came_stats[1:2, cols] * jnp.exp2(top_b - top)
        total = part_a + part_b
        inverse = 1.0 / total
        part_a, part_b = part_a * inverse, part_b * inverse
        mean_tan = part_a * tan_a + part_b * tan_b
        primal_a, primal_b = own[0, :, cols], came[0, :, cols].astype(jnp.float32)
        tangent_a, tangent_b = own[1, :, cols], came[1, :, cols].astype(jnp.float32)
        primal = part_a * primal_a + part_b * primal_b
        tangent = part_a * (tangent_a + (tan_a - mean_tan) * primal_a) + part_b * (
            tangent_b + (tan_b - mean_tan) * primal_b
        )
        sink[0, :, cols] = primal.astype(sink.dtype)
        sink[1, :, cols] = tangent.astype(sink.dtype)
        own_stats[0:1, cols] = top
        own_stats[1:2, cols] = total
        own_stats[2:3, cols] = mean_tan


def kernel(
    n_ctx,
    q_ref,
    k_ref,
    v_ref,
    qt_ref,
    kt_ref,
    vt_ref,
    tq_ref,
    tk_ref,
    cnt_ref,
    out_p,
    out_t,
    query,
    keyval,
    values_t,
    bias_own,
    bias_rows,
    bias,
    local,
    local_stats,
    sent,
    sent_stats,
    came,
    came_stats,
    outbuf,
    in_send,
    q_recv,
    kv_recv,
    zq_send,
    xq_send,
    fq_send,
    bias_send,
    bias_hop_send,
    bias_recv,
    part_send,
    part_recv,
    stat_send,
    stat_recv,
    out_send,
    out_recv,
):
    ctx = lax.axis_index("ctx")
    uly = lax.axis_index("uly")
    core = lax.rem(uly, 2)
    yh = lax.rem(ctx, 2)
    base = ctx - yh
    y = yh * 2 + lax.div(uly, 2)
    other = uly + 1 - 2 * core
    ahead = lax.rem(ctx + 2, n_ctx)
    behind = lax.rem(ctx + n_ctx - 2, n_ctx)
    behind_or_here = lax.rem(ctx + (1 - core) * (n_ctx - 2), n_ctx)
    here_or_ahead = lax.rem(ctx + core * 2, n_ctx)
    at_home = core == yh

    barrier = pltpu.get_barrier_semaphore()
    for step in range(1, 8):
        place = lax.rem(yh * 4 + uly + step, 8)
        pl.semaphore_signal(
            barrier, inc=1, device_id=(base + lax.div(place, 4), lax.rem(place, 4)), device_id_type=MESH
        )
    for where in (ahead, behind):
        for who in (uly, other):
            pl.semaphore_signal(barrier, inc=1, device_id=(where, who), device_id_type=MESH)

    lane = lax.broadcasted_iota(jnp.int32, (REACH * QT, MAXT), 1)
    code = lax.broadcasted_iota(jnp.int32, (REACH * QT, MAXT), 0)
    row = lax.broadcasted_iota(jnp.int32, (REACH * QT, 1), 0)
    usable = (lane < cnt_ref[0]) & (jnp.broadcast_to(tq_ref[...], code.shape) == uly)
    hit = usable & (jnp.broadcast_to(tk_ref[...], code.shape) == code)
    seen = jnp.max(jnp.where(hit, 1.0, 0.0), axis=1, keepdims=True)
    seen = jnp.maximum(seen, jnp.where(row == uly, 1.0, 0.0))
    bias_own[...] = jnp.broadcast_to((1.0 - seen) * NEG, (REACH * QT, HEAD))

    pl.semaphore_wait(barrier, 11)

    own_rows = pl.ds(pl.multiple_of(uly * TILE, TILE), TILE)
    low_half, high_half = pl.ds(0, HEAD), pl.ds(HEAD, HEAD)

    def group_device(place):
        return (base + lax.div(place, 2), lax.rem(place, 2) * 2 + yh)

    def send_in(moves, first, j):
        for step in range(4):
            place = lax.rem(y + step, 4)
            cols = pl.ds(pl.multiple_of((place * LOCAL_HEADS + j) * HEAD, HEAD), HEAD)

            def remote():
                for a, (src, dst, sem) in enumerate(moves):
                    pltpu.make_async_remote_copy(
                        src_ref=src.at[:, cols],
                        dst_ref=dst,
                        send_sem=in_send.at[step, first + a],
                        recv_sem=sem,
                        device_id=group_device(place),
                        device_id_type=MESH,
                    ).start()

            def stay():
                for src, dst, sem in moves:
                    pltpu.make_async_copy(src.at[:, cols], dst, sem).start()

            if step == 0:
                pl.when(at_home)(stay)
                pl.when(jnp.logical_not(at_home))(remote)
            else:
                remote()

    def send_q(j):
        send_in(
            (
                (q_ref, query.at[j, 0, own_rows, high_half], q_recv.at[j, 0]),
                (qt_ref, query.at[j, 0, own_rows, low_half], q_recv.at[j, 0]),
            ),
            0,
            j,
        )

    def send_kv(j):
        send_in(
            (
                (k_ref, keyval.at[j, 0, own_rows, low_half], kv_recv.at[j]),
                (kt_ref, keyval.at[j, 0, own_rows, high_half], kv_recv.at[j]),
                (v_ref, keyval.at[j, 1, own_rows, low_half], kv_recv.at[j]),
                (vt_ref, keyval.at[j, 1, own_rows, high_half], kv_recv.at[j]),
            ),
            2,
            j,
        )

    def bias_copy(step):
        return pltpu.make_async_remote_copy(
            src_ref=bias_own,
            dst_ref=bias_rows.at[0, uly],
            send_sem=bias_send.at[step],
            recv_sem=bias_recv.at[0],
            device_id=group_device(lax.rem(y + step, 4)),
            device_id_type=MESH,
        )

    def hop(j, src, dst, sems, ctx_to, uly_to):
        return pltpu.make_async_remote_copy(
            src_ref=query.at[j, src],
            dst_ref=query.at[j, dst],
            send_sem=sems.at[j],
            recv_sem=q_recv.at[j, dst],
            device_id=(ctx_to, uly_to),
            device_id_type=MESH,
        )

    def bias_hop(src, dst, way, ctx_to, uly_to):
        return pltpu.make_async_remote_copy(
            src_ref=bias_rows.at[src],
            dst_ref=bias_rows.at[dst],
            send_sem=bias_hop_send.at[way],
            recv_sem=bias_recv.at[dst],
            device_id=(ctx_to, uly_to),
            device_id_type=MESH,
        )

    def wait_query(j, slot):
        pltpu.make_async_copy(query.at[j, slot], query.at[j, slot], q_recv.at[j, slot]).wait()

    def wait_bias(slot):
        pltpu.make_async_copy(bias_rows.at[slot], bias_rows.at[slot], bias_recv.at[slot]).wait()

    def spread_bias(slot):
        for t in range(QT):
            for c in range(QT):
                at = slot * QT + c
                bias[slot, t, c] = jnp.broadcast_to(bias_rows[slot, t, at : at + 1, :], (8, HEAD))

    def forward_own(j):
        wait_query(j, 0)
        hop(j, 0, 2, zq_send, behind, uly).start()

        @pl.when(core == 1)
        def _():
            hop(j, 0, 1, xq_send, ctx, other).start()

        @pl.when(j == 0)
        def _():
            wait_bias(0)
            bias_hop(0, 2, 0, behind, uly).start()

            @pl.when(core == 1)
            def _():
                bias_hop(0, 1, 1, ctx, other).start()

            spread_bias(0)

    def forward_next(j):
        wait_query(j, 2)
        hop(j, 2, 3, fq_send, behind_or_here, other).start()

        @pl.when(core == 0)
        def _():
            hop(j, 2, 1, xq_send, ctx, other).start()

        @pl.when(j == 0)
        def _():
            wait_bias(2)
            bias_hop(2, 3, 2, behind_or_here, other).start()

            @pl.when(core == 0)
            def _():
                bias_hop(2, 1, 1, ctx, other).start()

            spread_bias(2)

    def part_copies(j, src, dst, ctx_to, uly_to):
        return [
            pltpu.make_async_remote_copy(
                src_ref=a.at[j, src],
                dst_ref=b.at[j, dst],
                send_sem=ss.at[j, src],
                recv_sem=rs.at[j, dst],
                device_id=(ctx_to, uly_to),
                device_id_type=MESH,
            )
            for a, b, ss, rs in (
                (sent, came, part_send, part_recv),
                (sent_stats, came_stats, stat_send, stat_recv),
            )
        ]

    def start_part(*args):
        for copy in part_copies(*args):
            copy.start()

    def wait_part(j, dst):
        pltpu.make_async_copy(came.at[j, dst], came.at[j, dst], part_recv.at[j, dst]).wait()
        pltpu.make_async_copy(came_stats.at[j, dst], came_stats.at[j, dst], stat_recv.at[j, dst]).wait()

    def work(j, slot):
        if slot % 2 == 0:
            sink, stats = local.at[j, slot // 2], local_stats.at[j, slot // 2]
        else:
            sink, stats = sent.at[j, slot // 2], sent_stats.at[j, slot // 2]
        attend(query, keyval, values_t, bias, j, slot, sink, stats)

    def absorb(j, which, dst, sink):
        merge(local.at[j, which], local_stats.at[j, which], came.at[j, dst], came_stats.at[j, dst], sink)

    def send_out(j):
        cols = pl.ds(pl.multiple_of((y * LOCAL_HEADS + j) * HEAD, HEAD), HEAD)
        for t in range(QT):
            def remote():
                for a, out in enumerate((out_p, out_t)):
                    pltpu.make_async_remote_copy(
                        src_ref=outbuf.at[j, a, pl.ds(t * TILE, TILE), :],
                        dst_ref=out.at[:, cols],
                        send_sem=out_send.at[t, a],
                        recv_sem=out_recv.at[a],
                        device_id=(base + core, t),
                        device_id_type=MESH,
                    ).start()

            def stay():
                for a, out in enumerate((out_p, out_t)):
                    pltpu.make_async_copy(
                        outbuf.at[j, a, pl.ds(t * TILE, TILE), :], out.at[:, cols], out_recv.at[a]
                    ).start()

            here = at_home & (uly == t)
            pl.when(here)(stay)
            pl.when(jnp.logical_not(here))(remote)

    @pl.when(at_home)
    def _():
        pltpu.make_async_copy(bias_own, bias_rows.at[0, uly], bias_recv.at[0]).start()

    @pl.when(jnp.logical_not(at_home))
    def _():
        bias_copy(0).start()

    for step in range(1, 4):
        bias_copy(step).start()
    def take_kv(j):
        pltpu.make_async_copy(keyval.at[j], keyval.at[j], kv_recv.at[j]).wait()
        values_t[j] = keyval[j, 1].T

    def work_from(j, slot):
        wait_query(j, slot)

        @pl.when(j == 0)
        def _():
            wait_bias(slot)
            spread_bias(slot)

        work(j, slot)

    @pl.loop(0, 2 * LOCAL_HEADS)
    def _(at):
        item = jnp.where(yh == 0, look_up(SEND_EVEN, at), look_up(SEND_ODD, at))
        j = item % 8
        pl.when(item < 8)(lambda: send_q(j))
        pl.when(item >= 8)(lambda: send_kv(j))

    @pl.loop(0, len(PLAN_EVEN))
    def _(at):
        item = jnp.where(core == 0, look_up(PLAN_EVEN, at), look_up(PLAN_ODD, at))
        j, what = item % 8, item // 8

        def attend_pass_previous():
            work_from(j, 1)
            start_part(j, 0, 1 - core, ctx, other)

        def attend_pass_far():
            work_from(j, 3)
            start_part(j, 1, core, here_or_ahead, other)

        def pass_on():
            @pl.when(core == 0)
            def _():
                wait_part(j, 1)
                absorb(j, 1, 1, local.at[j, 1])

            wait_part(j, 0)
            absorb(j, 1, 0, sent.at[j, 2])
            sent_stats[j, 2] = local_stats[j, 1]
            start_part(j, 2, 2, ahead, uly)

        def finish():
            @pl.when(core == 1)
            def _():
                wait_part(j, 1)
                absorb(j, 0, 1, local.at[j, 0])

            wait_part(j, 2)
            absorb(j, 0, 2, local.at[j, 0])
            outbuf[j, 0] = local[j, 0, 0].T.astype(jnp.bfloat16)
            outbuf[j, 1] = local[j, 0, 1].T.astype(jnp.bfloat16)
            send_out(j)

        steps = (
            lambda: forward_own(j),
            lambda: forward_next(j),
            lambda: take_kv(j),
            lambda: work(j, 0),
            attend_pass_previous,
            lambda: work(j, 2),
            attend_pass_far,
            pass_on,
            finish,
        )
        for number, step in enumerate(steps):
            pl.when(what == number)(step)

    group = pl.ds(0, LOCAL_HEADS * HEAD)
    for step in range(4):
        def gone():
            for a, src in enumerate((q_ref, qt_ref, k_ref, kt_ref, v_ref, vt_ref)):
                pltpu.make_async_copy(src.at[:, group], src.at[:, group], in_send.at[step, a]).wait()
            bias_copy(step).wait_send()

        if step == 0:
            pl.when(jnp.logical_not(at_home))(gone)
        else:
            gone()

    bias_hop(0, 2, 0, behind, uly).wait_send()
    bias_hop(0, 1, 1, ctx, other).wait_send()
    bias_hop(2, 3, 2, behind_or_here, other).wait_send()

    @pl.loop(0, LOCAL_HEADS)
    def _(j):
        hop(j, 0, 2, zq_send, behind, uly).wait_send()
        hop(j, 0, 1, xq_send, ctx, other).wait_send()
        hop(j, 2, 3, fq_send, behind_or_here, other).wait_send()
        for copy in (
            part_copies(j, 0, 1 - core, ctx, other)
            + part_copies(j, 1, core, here_or_ahead, other)
            + part_copies(j, 2, 2, ahead, uly)
        ):
            copy.wait_send()

    for t in range(QT):
        @pl.when(jnp.logical_not(at_home & (uly == t)))
        def _():
            for a, out in enumerate((out_p, out_t)):
                pltpu.make_async_copy(out.at[:, group], out.at[:, group], out_send.at[t, a]).wait()

    pltpu.make_async_copy(out_p, out_p, out_recv.at[0]).wait()
    pltpu.make_async_copy(out_t, out_t, out_recv.at[1]).wait()


def on_device(n_ctx, query_rows, key_rows, value_rows, query_tan, key_tan, value_tan, tile_query, tile_key, tile_count):
    heads = LOCAL_HEADS
    anyspace = pl.BlockSpec(memory_space=pl.ANY)
    vmem = pl.BlockSpec(memory_space=pltpu.VMEM)
    dma = pltpu.SemaphoreType.DMA
    return pl.pallas_call(
        functools.partial(kernel, n_ctx),
        out_shape=(
            jax.ShapeDtypeStruct(query_rows.shape, jnp.bfloat16),
            jax.ShapeDtypeStruct(query_rows.shape, jnp.bfloat16),
        ),
        in_specs=[anyspace] * 6 + [vmem, vmem, pl.BlockSpec(memory_space=pltpu.SMEM)],
        out_specs=(anyspace, anyspace),
        scratch_shapes=[
            pltpu.VMEM((heads, REACH, CT, 2 * HEAD), jnp.bfloat16),
            pltpu.VMEM((heads, 2, CT, 2 * HEAD), jnp.bfloat16),
            pltpu.VMEM((heads, 2 * HEAD, CT), jnp.bfloat16),
            pltpu.VMEM((REACH * QT, HEAD), jnp.float32),
            pltpu.VMEM((REACH, QT, REACH * QT, HEAD), jnp.float32),
            pltpu.VMEM((REACH, QT, QT, 8, HEAD), jnp.float32),
            pltpu.VMEM((heads, 2, 2, HEAD, CT), jnp.float32),
            pltpu.VMEM((heads, 2, 8, CT), jnp.float32),
            pltpu.VMEM((heads, 3, 2, HEAD, CT), jnp.bfloat16),
            pltpu.VMEM((heads, 3, 8, CT), jnp.float32),
            pltpu.VMEM((heads, 3, 2, HEAD, CT), jnp.bfloat16),
            pltpu.VMEM((heads, 3, 8, CT), jnp.float32),
            pltpu.VMEM((heads, 2, CT, HEAD), jnp.bfloat16),
            dma((4, 6)),
            dma((heads, REACH)),
            dma((heads,)),
            dma((heads,)),
            dma((heads,)),
            dma((heads,)),
            dma((4,)),
            dma((3,)),
            dma((REACH,)),
            dma((heads, 3)),
            dma((heads, 3)),
            dma((heads, 3)),
            dma((heads, 3)),
            dma((QT, 2)),
            dma((2,)),
        ],
        compiler_params=pltpu.CompilerParams(
            collective_id=0, has_side_effects=True, vmem_limit_bytes=60 * 1024 * 1024
        ),
        cost_estimate=pl.CostEstimate(
            flops=heads * CT * CT * REACH * HEAD * 12,
            bytes_accessed=12 * TILE * 2560,
            transcendentals=heads * CT * CT * REACH,
        ),
        name="band_attention",
    )(query_rows, key_rows, value_rows, query_tan, key_tan, value_tan, tile_query, tile_key, tile_count)


def solution(mesh):
    rows = P(("ctx", "uly"), None)
    return jax.shard_map(
        functools.partial(on_device, mesh.shape["ctx"]),
        mesh=mesh,
        in_specs=(rows,) * 6 + (P("ctx", None), P("ctx", None), P("ctx")),
        out_specs=(rows, rows),
        check_vma=False,
    )
```

```python
import functools
import math
import jax
import jax.numpy as jnp
from jax import lax
from jax.experimental import pallas as pl
from jax.experimental.pallas import tpu as pltpu
from jax.sharding import PartitionSpec as P

HEAD = 128
TILE = 128
REACH = 4
MAXT = 64
LOCAL_HEADS = 5
CT = 512
QT = 4
PART = 256
MESH = pl.DeviceIdType.MESH
SCALING = HEAD ** (-0.5)
LOG2E = math.log2(math.e)
NEG = -1e30


SEND_EVEN = [0, 8, 2, 1, 3, 4, 10, 9, 11, 12]
SEND_ODD = [2, 0, 8, 10, 9, 11, 3, 1, 4, 12]
PLAN_EVEN = [0, 8, 16, 2, 48, 1, 10, 40, 9, 32, 56, 24, 3, 18, 4, 50, 42, 11, 17, 58, 34, 41, 57, 12, 19, 43, 51, 26, 25, 66, 20, 49, 64, 28, 59, 35, 65, 52, 44, 33, 27, 36, 60, 67, 68]
PLAN_ODD = [0, 16, 8, 48, 40, 24, 56, 32, 2, 18, 50, 10, 17, 49, 42, 58, 34, 33, 3, 19, 35, 26, 1, 25, 11, 51, 43, 59, 4, 9, 20, 52, 64, 66, 41, 27, 57, 12, 44, 67, 28, 60, 36, 65, 68]


def look_up(table, at):
    words = [sum(v << (7 * n) for n, v in enumerate(table[w : w + 4])) for w in range(0, len(table), 4)]
    place = at // 4
    word = jnp.int32(words[0])
    for w in range(1, len(words)):
        word = jnp.where(place == w, jnp.int32(words[w]), word)
    return lax.shift_right_logical(word, (at % 4) * 7) % 128


def attend(query, keyval, values_t, bias, j, slot, sink, stats):
    per = PART // TILE
    nt = (((1,), (1,)), ((), ()))
    for h in range(CT // PART):
        cols = pl.ds(h * PART, PART)
        scores = lax.dot_general(
            keyval[j, 0, :, :HEAD], query[j, slot, cols, HEAD:], nt, preferred_element_type=jnp.float32
        )
        tans = lax.dot_general(
            keyval[j, 0], query[j, slot, cols, :], nt, preferred_element_type=jnp.float32
        )
        masked = []
        for c in range(QT):
            wide = jnp.concatenate([bias[slot, h * per + t, c] for t in range(per)], axis=1)
            masked.extend([wide] * (TILE // 8))
        scores = scores * (SCALING * LOG2E) + jnp.concatenate(masked, axis=0)
        top = jnp.max(scores, axis=0, keepdims=True)
        weights = jnp.exp2(scores - top)
        product = weights * tans
        total = jnp.sum(weights, axis=0, keepdims=True)
        inverse = 1.0 / total
        mean_tan = SCALING * jnp.sum(product, axis=0, keepdims=True) * inverse
        by_weight = jnp.dot(values_t[j], weights.astype(jnp.bfloat16), preferred_element_type=jnp.float32)
        by_product = jnp.dot(
            values_t[j, :HEAD, :], product.astype(jnp.bfloat16), preferred_element_type=jnp.float32
        )
        primal = by_weight[:HEAD] * inverse
        tangent = (SCALING * by_product + by_weight[HEAD:]) * inverse - mean_tan * primal
        sink[0, :, cols] = primal.astype(sink.dtype)
        sink[1, :, cols] = tangent.astype(sink.dtype)
        stats[0:1, cols] = top
        stats[1:2, cols] = total
        stats[2:3, cols] = mean_tan


def merge(own, own_stats, came, came_stats, sink):
    for h in range(CT // PART):
        cols = pl.ds(h * PART, PART)
        top_a, top_b = own_stats[0:1, cols], came_stats[0:1, cols]
        tan_a, tan_b = own_stats[2:3, cols], came_stats[2:3, cols]
        top = jnp.maximum(top_a, top_b)
        part_a = own_stats[1:2, cols] * jnp.exp2(top_a - top)
        part_b = came_stats[1:2, cols] * jnp.exp2(top_b - top)
        total = part_a + part_b
        inverse = 1.0 / total
        part_a, part_b = part_a * inverse, part_b * inverse
        mean_tan = part_a * tan_a + part_b * tan_b
        primal_a, primal_b = own[0, :, cols], came[0, :, cols].astype(jnp.float32)
        tangent_a, tangent_b = own[1, :, cols], came[1, :, cols].astype(jnp.float32)
        primal = part_a * primal_a + part_b * primal_b
        tangent = part_a * (tangent_a + (tan_a - mean_tan) * primal_a) + part_b * (
            tangent_b + (tan_b - mean_tan) * primal_b
        )
        sink[0, :, cols] = primal.astype(sink.dtype)
        sink[1, :, cols] = tangent.astype(sink.dtype)
        own_stats[0:1, cols] = top
        own_stats[1:2, cols] = total
        own_stats[2:3, cols] = mean_tan


def kernel(
    n_ctx,
    q_ref,
    k_ref,
    v_ref,
    qt_ref,
    kt_ref,
    vt_ref,
    tq_ref,
    tk_ref,
    cnt_ref,
    out_p,
    out_t,
    query,
    keyval,
    values_t,
    bias_own,
    bias_rows,
    bias,
    local,
    local_stats,
    sent,
    sent_stats,
    came,
    came_stats,
    outbuf,
    in_send,
    q_recv,
    kv_recv,
    zq_send,
    xq_send,
    fq_send,
    bias_send,
    bias_hop_send,
    bias_recv,
    part_send,
    part_recv,
    stat_send,
    stat_recv,
    out_send,
    out_recv,
    told,
):
    ctx = lax.axis_index("ctx")
    uly = lax.axis_index("uly")
    core = lax.rem(uly, 2)
    yh = lax.rem(ctx, 2)
    base = ctx - yh
    y = yh * 2 + lax.div(uly, 2)
    other = uly + 1 - 2 * core
    ahead = lax.rem(ctx + 2, n_ctx)
    behind = lax.rem(ctx + n_ctx - 2, n_ctx)
    behind_or_here = lax.rem(ctx + (1 - core) * (n_ctx - 2), n_ctx)
    here_or_ahead = lax.rem(ctx + core * 2, n_ctx)
    at_home = core == yh

    barrier = pltpu.get_barrier_semaphore()
    chip = uly - core
    for step in range(4):
        place = lax.rem(y + step, 4)

        def greet():
            pl.semaphore_signal(
                barrier, inc=1, device_id=(base + lax.div(place, 2), lax.rem(place, 2) * 2), device_id_type=MESH
            )

        if step == 0:
            pl.when(core == 1)(greet)
        else:
            greet()
    for where in (ahead, behind):
        pl.semaphore_signal(barrier, inc=1, device_id=(where, chip + 1), device_id_type=MESH)

    lane = lax.broadcasted_iota(jnp.int32, (REACH * QT, MAXT), 1)
    code = lax.broadcasted_iota(jnp.int32, (REACH * QT, MAXT), 0)
    row = lax.broadcasted_iota(jnp.int32, (REACH * QT, 1), 0)
    usable = (lane < cnt_ref[0]) & (jnp.broadcast_to(tq_ref[...], code.shape) == uly)
    hit = usable & (jnp.broadcast_to(tk_ref[...], code.shape) == code)
    seen = jnp.max(jnp.where(hit, 1.0, 0.0), axis=1, keepdims=True)
    seen = jnp.maximum(seen, jnp.where(row == uly, 1.0, 0.0))
    bias_own[...] = jnp.broadcast_to((1.0 - seen) * NEG, (REACH * QT, HEAD))

    @pl.when(core == 0)
    def _():
        pl.semaphore_wait(barrier, 7)
        pl.semaphore_signal(told, inc=1, device_id=(ctx, other), device_id_type=MESH)

    @pl.when(core == 1)
    def _():
        pl.semaphore_wait(told, 1)

    own_rows = pl.ds(pl.multiple_of(uly * TILE, TILE), TILE)
    low_half, high_half = pl.ds(0, HEAD), pl.ds(HEAD, HEAD)

    def group_device(place):
        return (base + lax.div(place, 2), lax.rem(place, 2) * 2 + yh)

    def send_in(moves, first, j):
        for step in range(4):
            place = lax.rem(y + step, 4)
            cols = pl.ds(pl.multiple_of((place * LOCAL_HEADS + j) * HEAD, HEAD), HEAD)

            def remote():
                for a, (src, dst, sem) in enumerate(moves):
                    pltpu.make_async_remote_copy(
                        src_ref=src.at[:, cols],
                        dst_ref=dst,
                        send_sem=in_send.at[step, first + a],
                        recv_sem=sem,
                        device_id=group_device(place),
                        device_id_type=MESH,
                    ).start()

            def stay():
                for src, dst, sem in moves:
                    pltpu.make_async_copy(src.at[:, cols], dst, sem).start()

            if step == 0:
                pl.when(at_home)(stay)
                pl.when(jnp.logical_not(at_home))(remote)
            else:
                remote()

    def send_q(j):
        send_in(
            (
                (q_ref, query.at[j, 0, own_rows, high_half], q_recv.at[j, 0]),
                (qt_ref, query.at[j, 0, own_rows, low_half], q_recv.at[j, 0]),
            ),
            0,
            j,
        )

    def send_kv(j):
        send_in(
            (
                (k_ref, keyval.at[j, 0, own_rows, low_half], kv_recv.at[j]),
                (kt_ref, keyval.at[j, 0, own_rows, high_half], kv_recv.at[j]),
                (v_ref, keyval.at[j, 1, own_rows, low_half], kv_recv.at[j]),
                (vt_ref, keyval.at[j, 1, own_rows, high_half], kv_recv.at[j]),
            ),
            2,
            j,
        )

    def bias_copy(step):
        return pltpu.make_async_remote_copy(
            src_ref=bias_own,
            dst_ref=bias_rows.at[0, uly],
            send_sem=bias_send.at[step],
            recv_sem=bias_recv.at[0],
            device_id=group_device(lax.rem(y + step, 4)),
            device_id_type=MESH,
        )

    def hop(j, src, dst, sems, ctx_to, uly_to):
        return pltpu.make_async_remote_copy(
            src_ref=query.at[j, src],
            dst_ref=query.at[j, dst],
            send_sem=sems.at[j],
            recv_sem=q_recv.at[j, dst],
            device_id=(ctx_to, uly_to),
            device_id_type=MESH,
        )

    def bias_hop(src, dst, way, ctx_to, uly_to):
        return pltpu.make_async_remote_copy(
            src_ref=bias_rows.at[src],
            dst_ref=bias_rows.at[dst],
            send_sem=bias_hop_send.at[way],
            recv_sem=bias_recv.at[dst],
            device_id=(ctx_to, uly_to),
            device_id_type=MESH,
        )

    def wait_query(j, slot):
        pltpu.make_async_copy(query.at[j, slot], query.at[j, slot], q_recv.at[j, slot]).wait()

    def wait_bias(slot):
        pltpu.make_async_copy(bias_rows.at[slot], bias_rows.at[slot], bias_recv.at[slot]).wait()

    def spread_bias(slot):
        for t in range(QT):
            for c in range(QT):
                at = slot * QT + c
                bias[slot, t, c] = jnp.broadcast_to(bias_rows[slot, t, at : at + 1, :], (8, HEAD))

    def forward_own(j):
        wait_query(j, 0)
        hop(j, 0, 2, zq_send, behind, uly).start()

        @pl.when(core == 1)
        def _():
            hop(j, 0, 1, xq_send, ctx, other).start()

        @pl.when(j == 0)
        def _():
            wait_bias(0)
            bias_hop(0, 2, 0, behind, uly).start()

            @pl.when(core == 1)
            def _():
                bias_hop(0, 1, 1, ctx, other).start()

            spread_bias(0)

    def forward_next(j):
        wait_query(j, 2)
        hop(j, 2, 3, fq_send, behind_or_here, other).start()

        @pl.when(core == 0)
        def _():
            hop(j, 2, 1, xq_send, ctx, other).start()

        @pl.when(j == 0)
        def _():
            wait_bias(2)
            bias_hop(2, 3, 2, behind_or_here, other).start()

            @pl.when(core == 0)
            def _():
                bias_hop(2, 1, 1, ctx, other).start()

            spread_bias(2)

    def part_copies(j, src, dst, ctx_to, uly_to):
        return [
            pltpu.make_async_remote_copy(
                src_ref=a.at[j, src],
                dst_ref=b.at[j, dst],
                send_sem=ss.at[j, src],
                recv_sem=rs.at[j, dst],
                device_id=(ctx_to, uly_to),
                device_id_type=MESH,
            )
            for a, b, ss, rs in (
                (sent, came, part_send, part_recv),
                (sent_stats, came_stats, stat_send, stat_recv),
            )
        ]

    def start_part(*args):
        for copy in part_copies(*args):
            copy.start()

    def wait_part(j, dst):
        pltpu.make_async_copy(came.at[j, dst], came.at[j, dst], part_recv.at[j, dst]).wait()
        pltpu.make_async_copy(came_stats.at[j, dst], came_stats.at[j, dst], stat_recv.at[j, dst]).wait()

    def work(j, slot):
        if slot % 2 == 0:
            sink, stats = local.at[j, slot // 2], local_stats.at[j, slot // 2]
        else:
            sink, stats = sent.at[j, slot // 2], sent_stats.at[j, slot // 2]
        attend(query, keyval, values_t, bias, j, slot, sink, stats)

    def absorb(j, which, dst, sink):
        merge(local.at[j, which], local_stats.at[j, which], came.at[j, dst], came_stats.at[j, dst], sink)

    def send_out(j):
        cols = pl.ds(pl.multiple_of((y * LOCAL_HEADS + j) * HEAD, HEAD), HEAD)
        for t in range(QT):
            def remote():
                for a, out in enumerate((out_p, out_t)):
                    pltpu.make_async_remote_copy(
                        src_ref=outbuf.at[j, a, pl.ds(t * TILE, TILE), :],
                        dst_ref=out.at[:, cols],
                        send_sem=out_send.at[t, a],
                        recv_sem=out_recv.at[a],
                        device_id=(base + core, t),
                        device_id_type=MESH,
                    ).start()

            def stay():
                for a, out in enumerate((out_p, out_t)):
                    pltpu.make_async_copy(
                        outbuf.at[j, a, pl.ds(t * TILE, TILE), :], out.at[:, cols], out_recv.at[a]
                    ).start()

            here = at_home & (uly == t)
            pl.when(here)(stay)
            pl.when(jnp.logical_not(here))(remote)

    @pl.when(at_home)
    def _():
        pltpu.make_async_copy(bias_own, bias_rows.at[0, uly], bias_recv.at[0]).start()

    @pl.when(jnp.logical_not(at_home))
    def _():
        bias_copy(0).start()

    for step in range(1, 4):
        bias_copy(step).start()
    def take_kv(j):
        pltpu.make_async_copy(keyval.at[j], keyval.at[j], kv_recv.at[j]).wait()
        values_t[j] = keyval[j, 1].T

    def work_from(j, slot):
        wait_query(j, slot)

        @pl.when(j == 0)
        def _():
            wait_bias(slot)
            spread_bias(slot)

        work(j, slot)

    @pl.loop(0, 2 * LOCAL_HEADS)
    def _(at):
        item = jnp.where(yh == 0, look_up(SEND_EVEN, at), look_up(SEND_ODD, at))
        j = item % 8
        pl.when(item < 8)(lambda: send_q(j))
        pl.when(item >= 8)(lambda: send_kv(j))

    @pl.when(core == 1)
    def _():
        pl.semaphore_wait(barrier, 4)
        pl.semaphore_signal(told, inc=1, device_id=(ctx, other), device_id_type=MESH)

    @pl.when(core == 0)
    def _():
        pl.semaphore_wait(told, 1)

    @pl.loop(0, len(PLAN_EVEN))
    def _(at):
        item = jnp.where(core == 0, look_up(PLAN_EVEN, at), look_up(PLAN_ODD, at))
        j, what = item % 8, item // 8

        def attend_pass_previous():
            work_from(j, 1)
            start_part(j, 0, 1 - core, ctx, other)

        def attend_pass_far():
            work_from(j, 3)
            start_part(j, 1, core, here_or_ahead, other)

        def pass_on():
            @pl.when(core == 0)
            def _():
                wait_part(j, 1)
                absorb(j, 1, 1, local.at[j, 1])

            wait_part(j, 0)
            absorb(j, 1, 0, sent.at[j, 2])
            sent_stats[j, 2] = local_stats[j, 1]
            start_part(j, 2, 2, ahead, uly)

        def finish():
            @pl.when(core == 1)
            def _():
                wait_part(j, 1)
                absorb(j, 0, 1, local.at[j, 0])

            wait_part(j, 2)
            absorb(j, 0, 2, local.at[j, 0])
            outbuf[j, 0] = local[j, 0, 0].T.astype(jnp.bfloat16)
            outbuf[j, 1] = local[j, 0, 1].T.astype(jnp.bfloat16)
            send_out(j)

        steps = (
            lambda: forward_own(j),
            lambda: forward_next(j),
            lambda: take_kv(j),
            lambda: work(j, 0),
            attend_pass_previous,
            lambda: work(j, 2),
            attend_pass_far,
            pass_on,
            finish,
        )
        for number, step in enumerate(steps):
            pl.when(what == number)(step)

    group = pl.ds(0, LOCAL_HEADS * HEAD)
    for step in range(4):
        def gone():
            for a, src in enumerate((q_ref, qt_ref, k_ref, kt_ref, v_ref, vt_ref)):
                pltpu.make_async_copy(src.at[:, group], src.at[:, group], in_send.at[step, a]).wait()
            bias_copy(step).wait_send()

        if step == 0:
            pl.when(jnp.logical_not(at_home))(gone)
        else:
            gone()

    bias_hop(0, 2, 0, behind, uly).wait_send()
    bias_hop(0, 1, 1, ctx, other).wait_send()
    bias_hop(2, 3, 2, behind_or_here, other).wait_send()

    @pl.loop(0, LOCAL_HEADS)
    def _(j):
        hop(j, 0, 2, zq_send, behind, uly).wait_send()
        hop(j, 0, 1, xq_send, ctx, other).wait_send()
        hop(j, 2, 3, fq_send, behind_or_here, other).wait_send()
        for copy in (
            part_copies(j, 0, 1 - core, ctx, other)
            + part_copies(j, 1, core, here_or_ahead, other)
            + part_copies(j, 2, 2, ahead, uly)
        ):
            copy.wait_send()

    for t in range(QT):
        @pl.when(jnp.logical_not(at_home & (uly == t)))
        def _():
            for a, out in enumerate((out_p, out_t)):
                pltpu.make_async_copy(out.at[:, group], out.at[:, group], out_send.at[t, a]).wait()

    pltpu.make_async_copy(out_p, out_p, out_recv.at[0]).wait()
    pltpu.make_async_copy(out_t, out_t, out_recv.at[1]).wait()


def on_device(n_ctx, query_rows, key_rows, value_rows, query_tan, key_tan, value_tan, tile_query, tile_key, tile_count):
    heads = LOCAL_HEADS
    anyspace = pl.BlockSpec(memory_space=pl.ANY)
    hbm = pl.BlockSpec(memory_space=pltpu.HBM)
    vmem = pl.BlockSpec(memory_space=pltpu.VMEM)
    dma = pltpu.SemaphoreType.DMA
    return pl.pallas_call(
        functools.partial(kernel, n_ctx),
        out_shape=(
            jax.ShapeDtypeStruct(query_rows.shape, jnp.bfloat16),
            jax.ShapeDtypeStruct(query_rows.shape, jnp.bfloat16),
        ),
        in_specs=[hbm] * 6 + [vmem, vmem, pl.BlockSpec(memory_space=pltpu.SMEM)],
        out_specs=(anyspace, anyspace),
        scratch_shapes=[
            pltpu.VMEM((heads, REACH, CT, 2 * HEAD), jnp.bfloat16),
            pltpu.VMEM((heads, 2, CT, 2 * HEAD), jnp.bfloat16),
            pltpu.VMEM((heads, 2 * HEAD, CT), jnp.bfloat16),
            pltpu.VMEM((REACH * QT, HEAD), jnp.float32),
            pltpu.VMEM((REACH, QT, REACH * QT, HEAD), jnp.float32),
            pltpu.VMEM((REACH, QT, QT, 8, HEAD), jnp.float32),
            pltpu.VMEM((heads, 2, 2, HEAD, CT), jnp.float32),
            pltpu.VMEM((heads, 2, 8, CT), jnp.float32),
            pltpu.VMEM((heads, 3, 2, HEAD, CT), jnp.bfloat16),
            pltpu.VMEM((heads, 3, 8, CT), jnp.float32),
            pltpu.VMEM((heads, 3, 2, HEAD, CT), jnp.bfloat16),
            pltpu.VMEM((heads, 3, 8, CT), jnp.float32),
            pltpu.VMEM((heads, 2, CT, HEAD), jnp.bfloat16),
            dma((4, 6)),
            dma((heads, REACH)),
            dma((heads,)),
            dma((heads,)),
            dma((heads,)),
            dma((heads,)),
            dma((4,)),
            dma((3,)),
            dma((REACH,)),
            dma((heads, 3)),
            dma((heads, 3)),
            dma((heads, 3)),
            dma((heads, 3)),
            dma((QT, 2)),
            dma((2,)),
            pltpu.SemaphoreType.REGULAR,
        ],
        compiler_params=pltpu.CompilerParams(
            collective_id=0, has_side_effects=True, vmem_limit_bytes=60 * 1024 * 1024
        ),
        cost_estimate=pl.CostEstimate(
            flops=heads * CT * CT * REACH * HEAD * 12,
            bytes_accessed=12 * TILE * 2560,
            transcendentals=heads * CT * CT * REACH,
        ),
        name="band_attention",
    )(query_rows, key_rows, value_rows, query_tan, key_tan, value_tan, tile_query, tile_key, tile_count)


def solution(mesh):
    rows = P(("ctx", "uly"), None)
    return jax.shard_map(
        functools.partial(on_device, mesh.shape["ctx"]),
        mesh=mesh,
        in_specs=(rows,) * 6 + (P("ctx", None), P("ctx", None), P("ctx")),
        out_specs=(rows, rows),
        check_vma=False,
    )
```

```python
import functools
import math
import jax
import jax.numpy as jnp
from jax import lax
from jax.experimental import pallas as pl
from jax.experimental.pallas import tpu as pltpu
from jax.sharding import PartitionSpec as P

HEAD = 128
TILE = 128
REACH = 4
MAXT = 64
LOCAL_HEADS = 5
CT = 512
QT = 4
PART = 256
MESH = pl.DeviceIdType.MESH
SCALING = HEAD ** (-0.5)
LOG2E = math.log2(math.e)
NEG = -1e30


MEET = [1, 0, 1, 0, 0]
SEND_EVEN = [4, 0, 8, 2, 3, 10, 12, 1, 11, 9]
SEND_ODD = [8, 0, 10, 12, 4, 2, 3, 11, 1, 9]
PLAN_EVEN = [0, 16, 4, 8, 24, 2, 40, 48, 12, 3, 32, 10, 18, 72, 42, 56, 74, 58, 20, 44, 26, 11, 60, 1, 52, 36, 50, 34, 28, 64, 9, 19, 51, 66, 35, 68, 43, 59, 27, 17, 33, 49, 41, 67, 57, 25, 65]
PLAN_ODD = [16, 48, 0, 18, 50, 8, 40, 32, 56, 20, 24, 52, 4, 2, 34, 26, 12, 3, 36, 44, 10, 42, 60, 11, 19, 43, 58, 64, 51, 28, 1, 27, 59, 35, 68, 66, 17, 49, 9, 25, 41, 67, 57, 33, 65, 80, 80]


def look_up(table, at):
    words = [sum(v << (7 * n) for n, v in enumerate(table[w : w + 4])) for w in range(0, len(table), 4)]
    place = at // 4
    word = jnp.int32(words[0])
    for w in range(1, len(words)):
        word = jnp.where(place == w, jnp.int32(words[w]), word)
    return lax.shift_right_logical(word, (at % 4) * 7) % 128


def attend(query, keys, values_t, bias, sink, stats):
    per = PART // TILE
    nt = (((1,), (1,)), ((), ()))
    for h in range(CT // PART):
        cols = pl.ds(h * PART, PART)
        scores = lax.dot_general(
            keys[:, :HEAD], query[cols, HEAD:], nt, preferred_element_type=jnp.float32
        )
        tans = lax.dot_general(
            keys[...], query[cols, :], nt, preferred_element_type=jnp.float32
        )
        masked = []
        for c in range(QT):
            wide = jnp.concatenate([bias[h * per + t, c] for t in range(per)], axis=1)
            masked.extend([wide] * (TILE // 8))
        scores = scores * (SCALING * LOG2E) + jnp.concatenate(masked, axis=0)
        top = jnp.max(scores, axis=0, keepdims=True)
        weights = jnp.exp2(scores - top)
        product = weights * tans
        total = jnp.sum(weights, axis=0, keepdims=True)
        inverse = 1.0 / total
        mean_tan = SCALING * jnp.sum(product, axis=0, keepdims=True) * inverse
        by_weight = jnp.dot(values_t[...], weights.astype(jnp.bfloat16), preferred_element_type=jnp.float32)
        by_product = jnp.dot(
            values_t[:HEAD, :], product.astype(jnp.bfloat16), preferred_element_type=jnp.float32
        )
        primal = by_weight[:HEAD] * inverse
        tangent = (SCALING * by_product + by_weight[HEAD:]) * inverse - mean_tan * primal
        sink[0, :, cols] = primal.astype(sink.dtype)
        sink[1, :, cols] = tangent.astype(sink.dtype)
        stats[3 * h : 3 * h + 1, :] = top
        stats[3 * h + 1 : 3 * h + 2, :] = total
        stats[3 * h + 2 : 3 * h + 3, :] = mean_tan


def merge(own, own_stats, came, came_stats, sink):
    for h in range(CT // PART):
        cols = pl.ds(h * PART, PART)
        top_a, top_b = own_stats[3 * h : 3 * h + 1, :], came_stats[3 * h : 3 * h + 1, :]
        tan_a, tan_b = own_stats[3 * h + 2 : 3 * h + 3, :], came_stats[3 * h + 2 : 3 * h + 3, :]
        top = jnp.maximum(top_a, top_b)
        part_a = own_stats[3 * h + 1 : 3 * h + 2, :] * jnp.exp2(top_a - top)
        part_b = came_stats[3 * h + 1 : 3 * h + 2, :] * jnp.exp2(top_b - top)
        total = part_a + part_b
        inverse = 1.0 / total
        part_a, part_b = part_a * inverse, part_b * inverse
        mean_tan = part_a * tan_a + part_b * tan_b
        primal_a, primal_b = own[0, :, cols], came[0, :, cols].astype(jnp.float32)
        tangent_a, tangent_b = own[1, :, cols], came[1, :, cols].astype(jnp.float32)
        primal = part_a * primal_a + part_b * primal_b
        tangent = part_a * (tangent_a + (tan_a - mean_tan) * primal_a) + part_b * (
            tangent_b + (tan_b - mean_tan) * primal_b
        )
        sink[0, :, cols] = primal.astype(sink.dtype)
        sink[1, :, cols] = tangent.astype(sink.dtype)
        own_stats[3 * h : 3 * h + 1, :] = top
        own_stats[3 * h + 1 : 3 * h + 2, :] = total
        own_stats[3 * h + 2 : 3 * h + 3, :] = mean_tan


def kernel(
    n_ctx,
    q_ref,
    k_ref,
    v_ref,
    qt_ref,
    kt_ref,
    vt_ref,
    tq_ref,
    tk_ref,
    cnt_ref,
    out_both,
    query,
    keyval,
    values_t,
    bias_own,
    bias_rows,
    bias,
    local,
    local_stats,
    sent,
    sent_stats,
    came,
    came_stats,
    outbuf,
    in_send,
    q_recv,
    kv_recv,
    zq_send,
    xq_send,
    fq_send,
    bias_send,
    bias_hop_send,
    bias_recv,
    part_send,
    part_recv,
    stat_send,
    stat_recv,
    out_send,
    out_recv,
    told,
    far_keyval,
    far_values_t,
    far_send,
    far_recv,
):
    out_p, out_t = out_both.at[0], out_both.at[1]
    ctx = lax.axis_index("ctx")
    uly = lax.axis_index("uly")
    core = lax.rem(uly, 2)
    yh = lax.rem(ctx, 2)
    base = ctx - yh
    y = yh * 2 + lax.div(uly, 2)
    other = uly + 1 - 2 * core
    ahead = lax.rem(ctx + 2, n_ctx)
    behind = lax.rem(ctx + n_ctx - 2, n_ctx)
    behind_or_here = lax.rem(ctx + (1 - core) * (n_ctx - 2), n_ctx)
    here_or_ahead = lax.rem(ctx + core * 2, n_ctx)
    at_home = core == yh

    barrier = pltpu.get_barrier_semaphore()
    chip = uly - core
    for step in range(4):
        place = lax.rem(y + step, 4)

        def greet():
            pl.semaphore_signal(
                barrier, inc=1, device_id=(base + lax.div(place, 2), lax.rem(place, 2) * 2), device_id_type=MESH
            )

        if step == 0:
            pl.when(core == 1)(greet)
        else:
            greet()
    for where in (ahead, behind):
        pl.semaphore_signal(barrier, inc=1, device_id=(where, chip + 1), device_id_type=MESH)

    lane = lax.broadcasted_iota(jnp.int32, (REACH * QT, MAXT), 1)
    code = lax.broadcasted_iota(jnp.int32, (REACH * QT, MAXT), 0)
    row = lax.broadcasted_iota(jnp.int32, (REACH * QT, 1), 0)
    usable = (lane < cnt_ref[0]) & (jnp.broadcast_to(tq_ref[...], code.shape) == uly)
    hit = usable & (jnp.broadcast_to(tk_ref[...], code.shape) == code)
    seen = jnp.max(jnp.where(hit, 1.0, 0.0), axis=1, keepdims=True)
    seen = jnp.maximum(seen, jnp.where(row == uly, 1.0, 0.0))
    bias_own[...] = jnp.broadcast_to((1.0 - seen) * NEG, (REACH * QT, HEAD))

    @pl.when(core == 0)
    def _():
        pl.semaphore_wait(barrier, 7)
        pl.semaphore_signal(told, inc=1, device_id=(ctx, other), device_id_type=MESH)

    @pl.when(core == 1)
    def _():
        pl.semaphore_wait(told, 1)

    own_rows = pl.ds(pl.multiple_of(uly * TILE, TILE), TILE)
    low_half, high_half = pl.ds(0, HEAD), pl.ds(HEAD, HEAD)

    def group_device(place):
        return (base + lax.div(place, 2), lax.rem(place, 2) * 2 + yh)

    def send_in(moves, first, j):
        for step in range(4):
            place = lax.rem(y + step, 4)
            cols = pl.ds(pl.multiple_of((place * LOCAL_HEADS + j) * HEAD, HEAD), HEAD)

            def remote():
                for a, (src, dst, sem) in enumerate(moves):
                    pltpu.make_async_remote_copy(
                        src_ref=src.at[:, cols],
                        dst_ref=dst,
                        send_sem=in_send.at[step, first + a],
                        recv_sem=sem,
                        device_id=group_device(place),
                        device_id_type=MESH,
                    ).start()

            def stay():
                for src, dst, sem in moves:
                    pltpu.make_async_copy(src.at[:, cols], dst, sem).start()

            if step == 0:
                pl.when(at_home)(stay)
                pl.when(jnp.logical_not(at_home))(remote)
            else:
                remote()

    def send_q(j):
        send_in(
            (
                (q_ref, query.at[j, 0, own_rows, high_half], q_recv.at[j, 0]),
                (qt_ref, query.at[j, 0, own_rows, low_half], q_recv.at[j, 0]),
            ),
            0,
            j,
        )

    def send_kv(j):
        send_in(
            (
                (k_ref, keyval.at[j, 0, own_rows, low_half], kv_recv.at[j]),
                (kt_ref, keyval.at[j, 0, own_rows, high_half], kv_recv.at[j]),
                (v_ref, keyval.at[j, 1, own_rows, low_half], kv_recv.at[j]),
                (vt_ref, keyval.at[j, 1, own_rows, high_half], kv_recv.at[j]),
            ),
            2,
            j,
        )

    def bias_copy(step):
        return pltpu.make_async_remote_copy(
            src_ref=bias_own,
            dst_ref=bias_rows.at[0, uly],
            send_sem=bias_send.at[step],
            recv_sem=bias_recv.at[0],
            device_id=group_device(lax.rem(y + step, 4)),
            device_id_type=MESH,
        )

    def hop(j, src, dst, sems, ctx_to, uly_to):
        return pltpu.make_async_remote_copy(
            src_ref=query.at[j, src],
            dst_ref=query.at[j, dst],
            send_sem=sems.at[j],
            recv_sem=q_recv.at[j, dst],
            device_id=(ctx_to, uly_to),
            device_id_type=MESH,
        )

    def bias_hop(src, dst, way, ctx_to, uly_to):
        return pltpu.make_async_remote_copy(
            src_ref=bias_rows.at[src],
            dst_ref=bias_rows.at[dst],
            send_sem=bias_hop_send.at[way],
            recv_sem=bias_recv.at[dst],
            device_id=(ctx_to, uly_to),
            device_id_type=MESH,
        )

    def wait_query(j, slot):
        pltpu.make_async_copy(query.at[j, slot], query.at[j, slot], q_recv.at[j, slot]).wait()

    def wait_bias(slot):
        pltpu.make_async_copy(bias_rows.at[slot], bias_rows.at[slot], bias_recv.at[slot]).wait()

    def spread_bias(slot, back, to):
        for t in range(QT):
            for c in range(QT):
                at = back * QT + c
                bias[to, t, c] = jnp.broadcast_to(bias_rows[slot, t, at : at + 1, :], (8, HEAD))

    def forward_own(j):
        wait_query(j, 0)
        hop(j, 0, 2, zq_send, behind, uly).start()

        @pl.when(core == 1)
        def _():
            hop(j, 0, 1, xq_send, ctx, other).start()

        @pl.when(j == 0)
        def _():
            wait_bias(0)
            bias_hop(0, 2, 0, behind, uly).start()

            @pl.when(core == 1)
            def _():
                bias_hop(0, 1, 1, ctx, other).start()

            spread_bias(0, 0, 0)

    def forward_next(j):
        wait_query(j, 2)

        @pl.when((core == 1) | far_by_query(j))
        def _():
            hop(j, 2, 3, fq_send, behind_or_here, other).start()

        @pl.when(core == 0)
        def _():
            hop(j, 2, 1, xq_send, ctx, other).start()

        @pl.when(j == 0)
        def _():
            wait_bias(2)
            bias_hop(2, 3, 2, behind_or_here, other).start()

            @pl.when(core == 0)
            def _():
                bias_hop(2, 1, 1, ctx, other).start()

            spread_bias(2, 2, 2)
            spread_bias(2, 3, REACH)

    def part_copies(j, src, dst, ctx_to, uly_to):
        return [
            pltpu.make_async_remote_copy(
                src_ref=a.at[j, src],
                dst_ref=b.at[j, dst],
                send_sem=ss.at[j, src],
                recv_sem=rs.at[j, dst],
                device_id=(ctx_to, uly_to),
                device_id_type=MESH,
            )
            for a, b, ss, rs in (
                (sent, came, part_send, part_recv),
                (sent_stats, came_stats, stat_send, stat_recv),
            )
        ]

    def start_part(*args):
        for copy in part_copies(*args):
            copy.start()

    def wait_part(j, dst):
        pltpu.make_async_copy(came.at[j, dst], came.at[j, dst], part_recv.at[j, dst]).wait()
        pltpu.make_async_copy(came_stats.at[j, dst], came_stats.at[j, dst], stat_recv.at[j, dst]).wait()

    def work(j, slot):
        if slot % 2 == 0:
            sink, stats = local.at[j, slot // 2], local_stats.at[j, slot // 2]
        else:
            sink, stats = sent.at[j, slot // 2], sent_stats.at[j, slot // 2]
        attend(query.at[j, slot], keyval.at[j, 0], values_t.at[j], bias.at[slot], sink, stats)

    def absorb(j, which, dst, sink):
        merge(local.at[j, which], local_stats.at[j, which], came.at[j, dst], came_stats.at[j, dst], sink)

    def send_out(j):
        cols = pl.ds(pl.multiple_of((y * LOCAL_HEADS + j) * HEAD, HEAD), HEAD)
        for t in range(QT):
            def remote():
                for a, out in enumerate((out_p, out_t)):
                    pltpu.make_async_remote_copy(
                        src_ref=outbuf.at[j, a, pl.ds(t * TILE, TILE), :],
                        dst_ref=out.at[:, cols],
                        send_sem=out_send.at[t, a],
                        recv_sem=out_recv.at[a],
                        device_id=(base + core, t),
                        device_id_type=MESH,
                    ).start()

            def stay():
                for a, out in enumerate((out_p, out_t)):
                    pltpu.make_async_copy(
                        outbuf.at[j, a, pl.ds(t * TILE, TILE), :], out.at[:, cols], out_recv.at[a]
                    ).start()

            here = at_home & (uly == t)
            pl.when(here)(stay)
            pl.when(jnp.logical_not(here))(remote)

    @pl.when(at_home)
    def _():
        pltpu.make_async_copy(bias_own, bias_rows.at[0, uly], bias_recv.at[0]).start()

    @pl.when(jnp.logical_not(at_home))
    def _():
        bias_copy(0).start()

    for step in range(1, 4):
        bias_copy(step).start()
    def far_by_query(j):
        return look_up(MEET, j) == 0

    def keys_ahead(j):
        return pltpu.make_async_remote_copy(
            src_ref=keyval.at[j],
            dst_ref=far_keyval.at[j],
            send_sem=far_send.at[j],
            recv_sem=far_recv.at[j],
            device_id=(ahead, other),
            device_id_type=MESH,
        )

    def take_kv(j):
        pltpu.make_async_copy(keyval.at[j], keyval.at[j], kv_recv.at[j]).wait()
        values_t[j] = keyval[j, 1].T

    def work_far(j):
        pltpu.make_async_copy(far_keyval.at[j], far_keyval.at[j], far_recv.at[j]).wait()
        far_values_t[...] = far_keyval[j, 1].T
        attend(
            query.at[j, 2], far_keyval.at[j, 0], far_values_t, bias.at[REACH], came.at[j, 1], came_stats.at[j, 1]
        )

    def work_from(j, slot, first):
        wait_query(j, slot)

        @pl.when(j == first)
        def _():
            wait_bias(slot)
            spread_bias(slot, slot, slot)

        work(j, slot)

    @pl.loop(0, 2 * LOCAL_HEADS)
    def _(at):
        item = jnp.where(yh == 0, look_up(SEND_EVEN, at), look_up(SEND_ODD, at))
        j = item % 8
        pl.when(item < 8)(lambda: send_q(j))
        pl.when(item >= 8)(lambda: send_kv(j))

    @pl.when(core == 1)
    def _():
        pl.semaphore_wait(barrier, 4)
        pl.semaphore_signal(told, inc=1, device_id=(ctx, other), device_id_type=MESH)

    @pl.when(core == 0)
    def _():
        pl.semaphore_wait(told, 1)

    @pl.loop(0, len(PLAN_EVEN))
    def _(at):
        item = jnp.where(core == 0, look_up(PLAN_EVEN, at), look_up(PLAN_ODD, at))
        j, what = item % 8, item // 8

        def attend_pass_previous():
            work_from(j, 1, jnp.where(core == 0, 0, 0))
            start_part(j, 0, 1 - core, ctx, other)

        def attend_pass_far():
            @pl.when((core == 0) | far_by_query(j))
            def _():
                work_from(j, 3, jnp.where(core == 0, 0, 4))
                start_part(j, 1, core, here_or_ahead, other)

            @pl.when((core == 1) & jnp.logical_not(far_by_query(j)))
            def _():
                keys_ahead(j).start()

        def pass_on():
            @pl.when((core == 0) & far_by_query(j))
            def _():
                wait_part(j, 1)

            @pl.when(core == 0)
            def _():
                absorb(j, 1, 1, local.at[j, 1])

            wait_part(j, 0)
            absorb(j, 1, 0, sent.at[j, 2])
            sent_stats[j, 2] = local_stats[j, 1]
            start_part(j, 2, 2, ahead, uly)

        def finish():
            @pl.when(core == 1)
            def _():
                wait_part(j, 1)
                absorb(j, 0, 1, local.at[j, 0])

            wait_part(j, 2)
            absorb(j, 0, 2, local.at[j, 0])
            outbuf[j, 0] = local[j, 0, 0].T.astype(jnp.bfloat16)
            outbuf[j, 1] = local[j, 0, 1].T.astype(jnp.bfloat16)
            send_out(j)

        steps = (
            lambda: forward_own(j),
            lambda: forward_next(j),
            lambda: take_kv(j),
            lambda: work(j, 0),
            attend_pass_previous,
            lambda: work(j, 2),
            attend_pass_far,
            pass_on,
            finish,
            lambda: work_far(j),
        )
        for number, step in enumerate(steps):
            pl.when(what == number)(step)

    group = pl.ds(0, LOCAL_HEADS * HEAD)
    for step in range(4):
        def gone():
            for a, src in enumerate((q_ref, qt_ref, k_ref, kt_ref, v_ref, vt_ref)):
                pltpu.make_async_copy(src.at[:, group], src.at[:, group], in_send.at[step, a]).wait()
            bias_copy(step).wait_send()

        if step == 0:
            pl.when(jnp.logical_not(at_home))(gone)
        else:
            gone()

    bias_hop(0, 2, 0, behind, uly).wait_send()
    bias_hop(0, 1, 1, ctx, other).wait_send()
    bias_hop(2, 3, 2, behind_or_here, other).wait_send()

    @pl.loop(0, LOCAL_HEADS)
    def _(j):
        hop(j, 0, 2, zq_send, behind, uly).wait_send()
        hop(j, 0, 1, xq_send, ctx, other).wait_send()

        @pl.when((core == 1) | far_by_query(j))
        def _():
            hop(j, 2, 3, fq_send, behind_or_here, other).wait_send()

        @pl.when((core == 0) | far_by_query(j))
        def _():
            for copy in part_copies(j, 1, core, here_or_ahead, other):
                copy.wait_send()

        @pl.when((core == 1) & jnp.logical_not(far_by_query(j)))
        def _():
            keys_ahead(j).wait_send()

        for copy in part_copies(j, 0, 1 - core, ctx, other) + part_copies(j, 2, 2, ahead, uly):
            copy.wait_send()

    for t in range(QT):
        @pl.when(jnp.logical_not(at_home & (uly == t)))
        def _():
            for a, out in enumerate((out_p, out_t)):
                pltpu.make_async_copy(out.at[:, group], out.at[:, group], out_send.at[t, a]).wait()

    pltpu.make_async_copy(out_p, out_p, out_recv.at[0]).wait()
    pltpu.make_async_copy(out_t, out_t, out_recv.at[1]).wait()


def on_device(n_ctx, query_rows, key_rows, value_rows, query_tan, key_tan, value_tan, tile_query, tile_key, tile_count):
    heads = LOCAL_HEADS
    anyspace = pl.BlockSpec(memory_space=pl.ANY)
    hbm = pl.BlockSpec(memory_space=pltpu.HBM)
    vmem = pl.BlockSpec(memory_space=pltpu.VMEM)
    dma = pltpu.SemaphoreType.DMA
    both = pl.pallas_call(
        functools.partial(kernel, n_ctx),
        out_shape=jax.ShapeDtypeStruct((2,) + query_rows.shape, jnp.bfloat16),
        in_specs=[hbm] * 6 + [vmem, vmem, pl.BlockSpec(memory_space=pltpu.SMEM)],
        out_specs=anyspace,
        scratch_shapes=[
            pltpu.VMEM((heads, REACH, CT, 2 * HEAD), jnp.bfloat16),
            pltpu.VMEM((heads, 2, CT, 2 * HEAD), jnp.bfloat16),
            pltpu.VMEM((heads, 2 * HEAD, CT), jnp.bfloat16),
            pltpu.VMEM((REACH * QT, HEAD), jnp.float32),
            pltpu.VMEM((REACH, QT, REACH * QT, HEAD), jnp.float32),
            pltpu.VMEM((REACH + 1, QT, QT, 8, HEAD), jnp.float32),
            pltpu.VMEM((heads, 2, 2, HEAD, CT), jnp.float32),
            pltpu.VMEM((heads, 2, 8, PART), jnp.float32),
            pltpu.VMEM((heads, 3, 2, HEAD, CT), jnp.bfloat16),
            pltpu.VMEM((heads, 3, 8, PART), jnp.float32),
            pltpu.VMEM((heads, 3, 2, HEAD, CT), jnp.bfloat16),
            pltpu.VMEM((heads, 3, 8, PART), jnp.float32),
            pltpu.VMEM((heads, 2, CT, HEAD), jnp.bfloat16),
            dma((4, 6)),
            dma((heads, REACH)),
            dma((heads,)),
            dma((heads,)),
            dma((heads,)),
            dma((heads,)),
            dma((4,)),
            dma((3,)),
            dma((REACH,)),
            dma((heads, 3)),
            dma((heads, 3)),
            dma((heads, 3)),
            dma((heads, 3)),
            dma((QT, 2)),
            dma((2,)),
            pltpu.SemaphoreType.REGULAR,
            pltpu.VMEM((heads, 2, CT, 2 * HEAD), jnp.bfloat16),
            pltpu.VMEM((2 * HEAD, CT), jnp.bfloat16),
            dma((heads,)),
            dma((heads,)),
        ],
        compiler_params=pltpu.CompilerParams(
            collective_id=0, has_side_effects=True, vmem_limit_bytes=60 * 1024 * 1024
        ),
        cost_estimate=pl.CostEstimate(
            flops=heads * CT * CT * REACH * HEAD * 12,
            bytes_accessed=12 * TILE * 2560,
            transcendentals=heads * CT * CT * REACH,
        ),
        name="band_attention",
    )(query_rows, key_rows, value_rows, query_tan, key_tan, value_tan, tile_query, tile_key, tile_count)
    return both[0], both[1]


def solution(mesh):
    rows = P(("ctx", "uly"), None)
    return jax.shard_map(
        functools.partial(on_device, mesh.shape["ctx"]),
        mesh=mesh,
        in_specs=(rows,) * 6 + (P("ctx", None), P("ctx", None), P("ctx")),
        out_specs=(rows, rows),
        check_vma=False,
    )
```

```python
import functools
import math
import jax
import jax.numpy as jnp
from jax import lax
from jax.experimental import pallas as pl
from jax.experimental.pallas import tpu as pltpu
from jax.sharding import PartitionSpec as P

HEAD = 128
TILE = 128
REACH = 4
MAXT = 64
LOCAL_HEADS = 5
CT = 512
QT = 4
PART = 256
HALVES = CT // PART
MESH = pl.DeviceIdType.MESH
SCALING = HEAD ** (-0.5)
LOG2E = math.log2(math.e)
NEG = -1e30


MEET = [1, 0, 1, 0, 0]
SEND_EVEN = [4, 0, 8, 2, 3, 10, 12, 1, 11, 9]
SEND_ODD = [8, 0, 10, 12, 4, 2, 3, 11, 1, 9]
PLAN_EVEN = [0, 16, 4, 8, 24, 2, 40, 48, 12, 3, 32, 10, 18, 72, 42, 56, 74, 58, 20, 44, 26, 11, 60, 1, 52, 36, 50, 34, 28, 64, 9, 19, 51, 66, 35, 68, 43, 59, 27, 17, 33, 49, 41, 67, 57, 25, 65]
PLAN_ODD = [16, 48, 0, 18, 50, 8, 40, 32, 56, 20, 24, 52, 4, 2, 34, 26, 12, 3, 36, 44, 10, 42, 60, 11, 19, 43, 58, 64, 51, 28, 1, 27, 59, 35, 68, 66, 17, 49, 9, 25, 41, 67, 57, 33, 65, 80, 80]


def look_up(table, at):
    words = [sum(v << (7 * n) for n, v in enumerate(table[w : w + 4])) for w in range(0, len(table), 4)]
    place = at // 4
    word = jnp.int32(words[0])
    for w in range(1, len(words)):
        word = jnp.where(place == w, jnp.int32(words[w]), word)
    return lax.shift_right_logical(word, (at % 4) * 7) % 128


def attend(h, query, keys, values_t, bias, sink, stats):
    per = PART // TILE
    nt = (((1,), (1,)), ((), ()))
    cols = pl.ds(h * PART, PART)
    scores = lax.dot_general(
        keys[:, :HEAD], query[cols, HEAD:], nt, preferred_element_type=jnp.float32
    )
    tans = lax.dot_general(
        keys[...], query[cols, :], nt, preferred_element_type=jnp.float32
    )
    masked = []
    for c in range(QT):
        wide = jnp.concatenate([bias[h * per + t, c] for t in range(per)], axis=1)
        masked.extend([wide] * (TILE // 8))
    scores = scores * (SCALING * LOG2E) + jnp.concatenate(masked, axis=0)
    top = jnp.max(scores, axis=0, keepdims=True)
    weights = jnp.exp2(scores - top)
    product = weights * tans
    total = jnp.sum(weights, axis=0, keepdims=True)
    inverse = 1.0 / total
    mean_tan = SCALING * jnp.sum(product, axis=0, keepdims=True) * inverse
    by_weight = jnp.dot(values_t[...], weights.astype(jnp.bfloat16), preferred_element_type=jnp.float32)
    by_product = jnp.dot(
        values_t[:HEAD, :], product.astype(jnp.bfloat16), preferred_element_type=jnp.float32
    )
    primal = by_weight[:HEAD] * inverse
    tangent = (SCALING * by_product + by_weight[HEAD:]) * inverse - mean_tan * primal
    sink[h, 0] = primal.astype(sink.dtype)
    sink[h, 1] = tangent.astype(sink.dtype)
    stats[h, 0:1, :] = top
    stats[h, 1:2, :] = total
    stats[h, 2:3, :] = mean_tan


def merge(h, own, own_stats, came, came_stats, sink):
    top_a, top_b = own_stats[h, 0:1, :], came_stats[h, 0:1, :]
    tan_a, tan_b = own_stats[h, 2:3, :], came_stats[h, 2:3, :]
    top = jnp.maximum(top_a, top_b)
    part_a = own_stats[h, 1:2, :] * jnp.exp2(top_a - top)
    part_b = came_stats[h, 1:2, :] * jnp.exp2(top_b - top)
    total = part_a + part_b
    inverse = 1.0 / total
    part_a, part_b = part_a * inverse, part_b * inverse
    mean_tan = part_a * tan_a + part_b * tan_b
    primal_a, primal_b = own[h, 0], came[h, 0].astype(jnp.float32)
    tangent_a, tangent_b = own[h, 1], came[h, 1].astype(jnp.float32)
    primal = part_a * primal_a + part_b * primal_b
    tangent = part_a * (tangent_a + (tan_a - mean_tan) * primal_a) + part_b * (
        tangent_b + (tan_b - mean_tan) * primal_b
    )
    sink[h, 0] = primal.astype(sink.dtype)
    sink[h, 1] = tangent.astype(sink.dtype)
    own_stats[h, 0:1, :] = top
    own_stats[h, 1:2, :] = total
    own_stats[h, 2:3, :] = mean_tan


def kernel(
    n_ctx,
    q_ref,
    k_ref,
    v_ref,
    qt_ref,
    kt_ref,
    vt_ref,
    tq_ref,
    tk_ref,
    cnt_ref,
    out_both,
    query,
    keyval,
    values_t,
    bias_own,
    bias_rows,
    bias,
    local,
    local_stats,
    sent,
    sent_stats,
    came,
    came_stats,
    outbuf,
    in_send,
    q_recv,
    kv_recv,
    zq_send,
    xq_send,
    fq_send,
    bias_send,
    bias_hop_send,
    bias_recv,
    part_send,
    part_recv,
    stat_send,
    stat_recv,
    out_send,
    out_recv,
    told,
    far_keyval,
    far_values_t,
    far_send,
    far_recv,
):
    out_p, out_t = out_both.at[0], out_both.at[1]
    ctx = lax.axis_index("ctx")
    uly = lax.axis_index("uly")
    core = lax.rem(uly, 2)
    yh = lax.rem(ctx, 2)
    base = ctx - yh
    y = yh * 2 + lax.div(uly, 2)
    other = uly + 1 - 2 * core
    ahead = lax.rem(ctx + 2, n_ctx)
    behind = lax.rem(ctx + n_ctx - 2, n_ctx)
    behind_or_here = lax.rem(ctx + (1 - core) * (n_ctx - 2), n_ctx)
    here_or_ahead = lax.rem(ctx + core * 2, n_ctx)
    at_home = core == yh

    barrier = pltpu.get_barrier_semaphore()
    chip = uly - core
    for step in range(4):
        place = lax.rem(y + step, 4)

        def greet():
            pl.semaphore_signal(
                barrier, inc=1, device_id=(base + lax.div(place, 2), lax.rem(place, 2) * 2), device_id_type=MESH
            )

        if step == 0:
            pl.when(core == 1)(greet)
        else:
            greet()
    for where in (ahead, behind):
        pl.semaphore_signal(barrier, inc=1, device_id=(where, chip + 1), device_id_type=MESH)

    lane = lax.broadcasted_iota(jnp.int32, (REACH * QT, MAXT), 1)
    code = lax.broadcasted_iota(jnp.int32, (REACH * QT, MAXT), 0)
    row = lax.broadcasted_iota(jnp.int32, (REACH * QT, 1), 0)
    usable = (lane < cnt_ref[0]) & (jnp.broadcast_to(tq_ref[...], code.shape) == uly)
    hit = usable & (jnp.broadcast_to(tk_ref[...], code.shape) == code)
    seen = jnp.max(jnp.where(hit, 1.0, 0.0), axis=1, keepdims=True)
    seen = jnp.maximum(seen, jnp.where(row == uly, 1.0, 0.0))
    bias_own[...] = jnp.broadcast_to((1.0 - seen) * NEG, (REACH * QT, HEAD))

    @pl.when(core == 0)
    def _():
        pl.semaphore_wait(barrier, 7)
        pl.semaphore_signal(told, inc=1, device_id=(ctx, other), device_id_type=MESH)

    @pl.when(core == 1)
    def _():
        pl.semaphore_wait(told, 1)

    own_rows = pl.ds(pl.multiple_of(uly * TILE, TILE), TILE)
    low_half, high_half = pl.ds(0, HEAD), pl.ds(HEAD, HEAD)

    def group_device(place):
        return (base + lax.div(place, 2), lax.rem(place, 2) * 2 + yh)

    def send_in(moves, first, j):
        for step in range(4):
            place = lax.rem(y + step, 4)
            cols = pl.ds(pl.multiple_of((place * LOCAL_HEADS + j) * HEAD, HEAD), HEAD)

            def remote():
                for a, (src, dst, sem) in enumerate(moves):
                    pltpu.make_async_remote_copy(
                        src_ref=src.at[:, cols],
                        dst_ref=dst,
                        send_sem=in_send.at[step, first + a],
                        recv_sem=sem,
                        device_id=group_device(place),
                        device_id_type=MESH,
                    ).start()

            def stay():
                for src, dst, sem in moves:
                    pltpu.make_async_copy(src.at[:, cols], dst, sem).start()

            if step == 0:
                pl.when(at_home)(stay)
                pl.when(jnp.logical_not(at_home))(remote)
            else:
                remote()

    def send_q(j):
        send_in(
            (
                (q_ref, query.at[j, 0, own_rows, high_half], q_recv.at[j, 0]),
                (qt_ref, query.at[j, 0, own_rows, low_half], q_recv.at[j, 0]),
            ),
            0,
            j,
        )

    def send_kv(j):
        send_in(
            (
                (k_ref, keyval.at[j, 0, own_rows, low_half], kv_recv.at[j]),
                (kt_ref, keyval.at[j, 0, own_rows, high_half], kv_recv.at[j]),
                (v_ref, keyval.at[j, 1, own_rows, low_half], kv_recv.at[j]),
                (vt_ref, keyval.at[j, 1, own_rows, high_half], kv_recv.at[j]),
            ),
            2,
            j,
        )

    def bias_copy(step):
        return pltpu.make_async_remote_copy(
            src_ref=bias_own,
            dst_ref=bias_rows.at[0, uly],
            send_sem=bias_send.at[step],
            recv_sem=bias_recv.at[0],
            device_id=group_device(lax.rem(y + step, 4)),
            device_id_type=MESH,
        )

    def hop(j, src, dst, sems, ctx_to, uly_to):
        return pltpu.make_async_remote_copy(
            src_ref=query.at[j, src],
            dst_ref=query.at[j, dst],
            send_sem=sems.at[j],
            recv_sem=q_recv.at[j, dst],
            device_id=(ctx_to, uly_to),
            device_id_type=MESH,
        )

    def bias_hop(src, dst, way, ctx_to, uly_to):
        return pltpu.make_async_remote_copy(
            src_ref=bias_rows.at[src],
            dst_ref=bias_rows.at[dst],
            send_sem=bias_hop_send.at[way],
            recv_sem=bias_recv.at[dst],
            device_id=(ctx_to, uly_to),
            device_id_type=MESH,
        )

    def wait_query(j, slot):
        pltpu.make_async_copy(query.at[j, slot], query.at[j, slot], q_recv.at[j, slot]).wait()

    def wait_bias(slot):
        pltpu.make_async_copy(bias_rows.at[slot], bias_rows.at[slot], bias_recv.at[slot]).wait()

    def spread_bias(slot, back, to):
        for t in range(QT):
            for c in range(QT):
                at = back * QT + c
                bias[to, t, c] = jnp.broadcast_to(bias_rows[slot, t, at : at + 1, :], (8, HEAD))

    def forward_own(j):
        wait_query(j, 0)
        hop(j, 0, 2, zq_send, behind, uly).start()

        @pl.when(core == 1)
        def _():
            hop(j, 0, 1, xq_send, ctx, other).start()

        @pl.when(j == 0)
        def _():
            wait_bias(0)
            bias_hop(0, 2, 0, behind, uly).start()

            @pl.when(core == 1)
            def _():
                bias_hop(0, 1, 1, ctx, other).start()

            spread_bias(0, 0, 0)

    def forward_next(j):
        wait_query(j, 2)

        @pl.when((core == 1) | far_by_query(j))
        def _():
            hop(j, 2, 3, fq_send, behind_or_here, other).start()

        @pl.when(core == 0)
        def _():
            hop(j, 2, 1, xq_send, ctx, other).start()

        @pl.when(j == 0)
        def _():
            wait_bias(2)
            bias_hop(2, 3, 2, behind_or_here, other).start()

            @pl.when(core == 0)
            def _():
                bias_hop(2, 1, 1, ctx, other).start()

            spread_bias(2, 2, 2)
            spread_bias(2, 3, REACH)

    def part_copies(h, j, src, dst, ctx_to, uly_to):
        return [
            pltpu.make_async_remote_copy(
                src_ref=a.at[j, src, h],
                dst_ref=b.at[j, dst, h],
                send_sem=ss.at[j, src, h],
                recv_sem=rs.at[j, dst, h],
                device_id=(ctx_to, uly_to),
                device_id_type=MESH,
            )
            for a, b, ss, rs in (
                (sent, came, part_send, part_recv),
                (sent_stats, came_stats, stat_send, stat_recv),
            )
        ]

    def start_part(*args):
        for copy in part_copies(*args):
            copy.start()

    def wait_part(h, j, dst):
        for ref, sem in ((came, part_recv), (came_stats, stat_recv)):
            pltpu.make_async_copy(ref.at[j, dst, h], ref.at[j, dst, h], sem.at[j, dst, h]).wait()

    def work(j, slot, *way):
        kept = slot % 2 == 0
        place = (j, slot // 2)
        sink, stats = (local, local_stats) if kept else (sent, sent_stats)
        for h in range(HALVES):
            attend(
                h,
                query.at[j, slot],
                keyval.at[j, 0],
                values_t.at[j],
                bias.at[slot],
                sink.at[place],
                stats.at[place],
            )
            if not kept:
                start_part(h, j, slot // 2, *way)

    def absorb(h, j, which, dst, sink):
        merge(h, local.at[j, which], local_stats.at[j, which], came.at[j, dst], came_stats.at[j, dst], sink)

    def send_out(h, j):
        cols = pl.ds(pl.multiple_of((y * LOCAL_HEADS + j) * HEAD, HEAD), HEAD)
        for t in range(h * PART // TILE, (h + 1) * PART // TILE):
            def remote():
                for a, out in enumerate((out_p, out_t)):
                    pltpu.make_async_remote_copy(
                        src_ref=outbuf.at[j, a, pl.ds(t * TILE, TILE), :],
                        dst_ref=out.at[:, cols],
                        send_sem=out_send.at[t, a],
                        recv_sem=out_recv.at[a],
                        device_id=(base + core, t),
                        device_id_type=MESH,
                    ).start()

            def stay():
                for a, out in enumerate((out_p, out_t)):
                    pltpu.make_async_copy(
                        outbuf.at[j, a, pl.ds(t * TILE, TILE), :], out.at[:, cols], out_recv.at[a]
                    ).start()

            here = at_home & (uly == t)
            pl.when(here)(stay)
            pl.when(jnp.logical_not(here))(remote)

    @pl.when(at_home)
    def _():
        pltpu.make_async_copy(bias_own, bias_rows.at[0, uly], bias_recv.at[0]).start()

    @pl.when(jnp.logical_not(at_home))
    def _():
        bias_copy(0).start()

    for step in range(1, 4):
        bias_copy(step).start()
    def far_by_query(j):
        return look_up(MEET, j) == 0

    def keys_ahead(j):
        return pltpu.make_async_remote_copy(
            src_ref=keyval.at[j],
            dst_ref=far_keyval.at[j],
            send_sem=far_send.at[j],
            recv_sem=far_recv.at[j],
            device_id=(ahead, other),
            device_id_type=MESH,
        )

    def take_kv(j):
        pltpu.make_async_copy(keyval.at[j], keyval.at[j], kv_recv.at[j]).wait()
        values_t[j] = keyval[j, 1].T

    def work_far(j):
        pltpu.make_async_copy(far_keyval.at[j], far_keyval.at[j], far_recv.at[j]).wait()
        far_values_t[...] = far_keyval[j, 1].T
        for h in range(HALVES):
            attend(
                h,
                query.at[j, 2],
                far_keyval.at[j, 0],
                far_values_t,
                bias.at[REACH],
                came.at[j, 1],
                came_stats.at[j, 1],
            )

    def work_from(j, slot, first, *way):
        wait_query(j, slot)

        @pl.when(j == first)
        def _():
            wait_bias(slot)
            spread_bias(slot, slot, slot)

        work(j, slot, *way)

    @pl.loop(0, 2 * LOCAL_HEADS)
    def _(at):
        item = jnp.where(yh == 0, look_up(SEND_EVEN, at), look_up(SEND_ODD, at))
        j = item % 8
        pl.when(item < 8)(lambda: send_q(j))
        pl.when(item >= 8)(lambda: send_kv(j))

    @pl.when(core == 1)
    def _():
        pl.semaphore_wait(barrier, 4)
        pl.semaphore_signal(told, inc=1, device_id=(ctx, other), device_id_type=MESH)

    @pl.when(core == 0)
    def _():
        pl.semaphore_wait(told, 1)

    @pl.loop(0, len(PLAN_EVEN))
    def _(at):
        item = jnp.where(core == 0, look_up(PLAN_EVEN, at), look_up(PLAN_ODD, at))
        j, what = item % 8, item // 8

        def attend_pass_previous():
            work_from(j, 1, jnp.where(core == 0, 0, 0), 1 - core, ctx, other)

        def attend_pass_far():
            @pl.when((core == 0) | far_by_query(j))
            def _():
                work_from(j, 3, jnp.where(core == 0, 0, 4), core, here_or_ahead, other)

            @pl.when((core == 1) & jnp.logical_not(far_by_query(j)))
            def _():
                keys_ahead(j).start()

        def pass_on():
            for h in range(HALVES):
                @pl.when((core == 0) & far_by_query(j))
                def _():
                    wait_part(h, j, 1)

                @pl.when(core == 0)
                def _():
                    absorb(h, j, 1, 1, local.at[j, 1])

                wait_part(h, j, 0)
                absorb(h, j, 1, 0, sent.at[j, 2])
                sent_stats[j, 2, h] = local_stats[j, 1, h]
                start_part(h, j, 2, 2, ahead, uly)

        def finish():
            for h in range(HALVES):
                @pl.when(core == 1)
                def _():
                    wait_part(h, j, 1)
                    absorb(h, j, 0, 1, local.at[j, 0])

                wait_part(h, j, 2)
                absorb(h, j, 0, 2, local.at[j, 0])
                rows = pl.ds(h * PART, PART)
                outbuf[j, 0, rows, :] = local[j, 0, h, 0].T.astype(jnp.bfloat16)
                outbuf[j, 1, rows, :] = local[j, 0, h, 1].T.astype(jnp.bfloat16)
                send_out(h, j)

        steps = (
            lambda: forward_own(j),
            lambda: forward_next(j),
            lambda: take_kv(j),
            lambda: work(j, 0),
            attend_pass_previous,
            lambda: work(j, 2),
            attend_pass_far,
            pass_on,
            finish,
            lambda: work_far(j),
        )
        for number, step in enumerate(steps):
            pl.when(what == number)(step)

    group = pl.ds(0, LOCAL_HEADS * HEAD)
    for step in range(4):
        def gone():
            for a, src in enumerate((q_ref, qt_ref, k_ref, kt_ref, v_ref, vt_ref)):
                pltpu.make_async_copy(src.at[:, group], src.at[:, group], in_send.at[step, a]).wait()
            bias_copy(step).wait_send()

        if step == 0:
            pl.when(jnp.logical_not(at_home))(gone)
        else:
            gone()

    bias_hop(0, 2, 0, behind, uly).wait_send()
    bias_hop(0, 1, 1, ctx, other).wait_send()
    bias_hop(2, 3, 2, behind_or_here, other).wait_send()

    @pl.loop(0, LOCAL_HEADS)
    def _(j):
        hop(j, 0, 2, zq_send, behind, uly).wait_send()
        hop(j, 0, 1, xq_send, ctx, other).wait_send()

        @pl.when((core == 1) | far_by_query(j))
        def _():
            hop(j, 2, 3, fq_send, behind_or_here, other).wait_send()

        @pl.when((core == 0) | far_by_query(j))
        def _():
            for h in range(HALVES):
                for copy in part_copies(h, j, 1, core, here_or_ahead, other):
                    copy.wait_send()

        @pl.when((core == 1) & jnp.logical_not(far_by_query(j)))
        def _():
            keys_ahead(j).wait_send()

        for h in range(HALVES):
            for copy in part_copies(h, j, 0, 1 - core, ctx, other) + part_copies(h, j, 2, 2, ahead, uly):
                copy.wait_send()

    for t in range(QT):
        @pl.when(jnp.logical_not(at_home & (uly == t)))
        def _():
            for a, out in enumerate((out_p, out_t)):
                pltpu.make_async_copy(out.at[:, group], out.at[:, group], out_send.at[t, a]).wait()

    pltpu.make_async_copy(out_p, out_p, out_recv.at[0]).wait()
    pltpu.make_async_copy(out_t, out_t, out_recv.at[1]).wait()


def on_device(n_ctx, query_rows, key_rows, value_rows, query_tan, key_tan, value_tan, tile_query, tile_key, tile_count):
    heads = LOCAL_HEADS
    anyspace = pl.BlockSpec(memory_space=pl.ANY)
    hbm = pl.BlockSpec(memory_space=pltpu.HBM)
    vmem = pl.BlockSpec(memory_space=pltpu.VMEM)
    dma = pltpu.SemaphoreType.DMA
    both = pl.pallas_call(
        functools.partial(kernel, n_ctx),
        out_shape=jax.ShapeDtypeStruct((2,) + query_rows.shape, jnp.bfloat16),
        in_specs=[hbm] * 6 + [vmem, vmem, pl.BlockSpec(memory_space=pltpu.SMEM)],
        out_specs=anyspace,
        scratch_shapes=[
            pltpu.VMEM((heads, REACH, CT, 2 * HEAD), jnp.bfloat16),
            pltpu.VMEM((heads, 2, CT, 2 * HEAD), jnp.bfloat16),
            pltpu.VMEM((heads, 2 * HEAD, CT), jnp.bfloat16),
            pltpu.VMEM((REACH * QT, HEAD), jnp.float32),
            pltpu.VMEM((REACH, QT, REACH * QT, HEAD), jnp.float32),
            pltpu.VMEM((REACH + 1, QT, QT, 8, HEAD), jnp.float32),
            pltpu.VMEM((heads, 2, HALVES, 2, HEAD, PART), jnp.float32),
            pltpu.VMEM((heads, 2, HALVES, 8, PART), jnp.float32),
            pltpu.VMEM((heads, 3, HALVES, 2, HEAD, PART), jnp.bfloat16),
            pltpu.VMEM((heads, 3, HALVES, 8, PART), jnp.float32),
            pltpu.VMEM((heads, 3, HALVES, 2, HEAD, PART), jnp.bfloat16),
            pltpu.VMEM((heads, 3, HALVES, 8, PART), jnp.float32),
            pltpu.VMEM((heads, 2, CT, HEAD), jnp.bfloat16),
            dma((4, 6)),
            dma((heads, REACH)),
            dma((heads,)),
            dma((heads,)),
            dma((heads,)),
            dma((heads,)),
            dma((4,)),
            dma((3,)),
            dma((REACH,)),
            dma((heads, 3, HALVES)),
            dma((heads, 3, HALVES)),
            dma((heads, 3, HALVES)),
            dma((heads, 3, HALVES)),
            dma((QT, 2)),
            dma((2,)),
            pltpu.SemaphoreType.REGULAR,
            pltpu.VMEM((heads, 2, CT, 2 * HEAD), jnp.bfloat16),
            pltpu.VMEM((2 * HEAD, CT), jnp.bfloat16),
            dma((heads,)),
            dma((heads,)),
        ],
        compiler_params=pltpu.CompilerParams(
            collective_id=0, has_side_effects=True, vmem_limit_bytes=60 * 1024 * 1024
        ),
        cost_estimate=pl.CostEstimate(
            flops=heads * CT * CT * REACH * HEAD * 12,
            bytes_accessed=12 * TILE * 2560,
            transcendentals=heads * CT * CT * REACH,
        ),
        name="band_attention",
    )(query_rows, key_rows, value_rows, query_tan, key_tan, value_tan, tile_query, tile_key, tile_count)
    return both[0], both[1]


def solution(mesh):
    rows = P(("ctx", "uly"), None)
    return jax.shard_map(
        functools.partial(on_device, mesh.shape["ctx"]),
        mesh=mesh,
        in_specs=(rows,) * 6 + (P("ctx", None), P("ctx", None), P("ctx")),
        out_specs=(rows, rows),
        check_vma=False,
    )
```

```python
import functools
import math
import jax
import jax.numpy as jnp
from jax import lax
from jax.experimental import pallas as pl
from jax.experimental.pallas import tpu as pltpu
from jax.sharding import PartitionSpec as P

HEAD = 128
TILE = 128
REACH = 4
MAXT = 64
LOCAL_HEADS = 5
CT = 512
QT = 4
PART = 256
HALVES = CT // PART
MESH = pl.DeviceIdType.MESH
SCALING = HEAD ** (-0.5)
LOG2E = math.log2(math.e)
NEG = -1e30


MEET = [1, 0, 0, 1, 0]
SEND_EVEN = [0, 4, 8, 2, 12, 1, 3, 9, 10, 11]
SEND_ODD = [8, 0, 11, 4, 12, 10, 1, 9, 3, 2]
PLAN_EVEN = [0, 4, 16, 8, 12, 2, 32, 40, 48, 72, 56, 1, 20, 10, 24, 52, 9, 28, 36, 44, 17, 33, 25, 60, 18, 3, 42, 58, 26, 64, 49, 68, 19, 27, 41, 57, 51, 11, 66, 50, 75, 35, 43, 65, 59, 34, 67]
PLAN_ODD = [16, 48, 0, 19, 51, 8, 40, 32, 4, 56, 24, 12, 20, 52, 44, 36, 60, 18, 1, 50, 28, 34, 9, 17, 49, 3, 41, 33, 2, 68, 57, 11, 64, 43, 10, 42, 59, 25, 65, 26, 58, 35, 27, 67, 66, 80, 80]


def look_up(table, at):
    words = [sum(v << (7 * n) for n, v in enumerate(table[w : w + 4])) for w in range(0, len(table), 4)]
    place = at // 4
    word = jnp.int32(words[0])
    for w in range(1, len(words)):
        word = jnp.where(place == w, jnp.int32(words[w]), word)
    return lax.shift_right_logical(word, (at % 4) * 7) % 128


def attend(h, query, keys, values_t, bias, sink, stats):
    per = PART // TILE
    nt = (((1,), (1,)), ((), ()))
    cols = pl.ds(h * PART, PART)
    scores = lax.dot_general(
        keys[:, :HEAD], query[cols, HEAD:], nt, preferred_element_type=jnp.float32
    )
    tans = lax.dot_general(
        keys[...], query[cols, :], nt, preferred_element_type=jnp.float32
    )
    masked = []
    for c in range(QT):
        wide = jnp.concatenate([bias[h * per + t, c] for t in range(per)], axis=1)
        masked.extend([wide] * (TILE // 8))
    scores = scores * (SCALING * LOG2E) + jnp.concatenate(masked, axis=0)
    top = jnp.max(scores, axis=0, keepdims=True)
    weights = jnp.exp2(scores - top)
    product = weights * tans
    total = jnp.sum(weights, axis=0, keepdims=True)
    inverse = 1.0 / total
    mean_tan = SCALING * jnp.sum(product, axis=0, keepdims=True) * inverse
    by_weight = jnp.dot(values_t[...], weights.astype(jnp.bfloat16), preferred_element_type=jnp.float32)
    by_product = jnp.dot(
        values_t[:HEAD, :], product.astype(jnp.bfloat16), preferred_element_type=jnp.float32
    )
    primal = by_weight[:HEAD] * inverse
    tangent = (SCALING * by_product + by_weight[HEAD:]) * inverse - mean_tan * primal
    sink[h, 0] = primal.astype(sink.dtype)
    sink[h, 1] = tangent.astype(sink.dtype)
    stats[h, 0:1, :] = top
    stats[h, 1:2, :] = total
    stats[h, 2:3, :] = mean_tan


def merge(h, own, own_stats, came, came_stats, sink):
    top_a, top_b = own_stats[h, 0:1, :], came_stats[h, 0:1, :]
    tan_a, tan_b = own_stats[h, 2:3, :], came_stats[h, 2:3, :]
    top = jnp.maximum(top_a, top_b)
    part_a = own_stats[h, 1:2, :] * jnp.exp2(top_a - top)
    part_b = came_stats[h, 1:2, :] * jnp.exp2(top_b - top)
    total = part_a + part_b
    inverse = 1.0 / total
    part_a, part_b = part_a * inverse, part_b * inverse
    mean_tan = part_a * tan_a + part_b * tan_b
    primal_a, primal_b = own[h, 0], came[h, 0].astype(jnp.float32)
    tangent_a, tangent_b = own[h, 1], came[h, 1].astype(jnp.float32)
    primal = part_a * primal_a + part_b * primal_b
    tangent = part_a * (tangent_a + (tan_a - mean_tan) * primal_a) + part_b * (
        tangent_b + (tan_b - mean_tan) * primal_b
    )
    sink[h, 0] = primal.astype(sink.dtype)
    sink[h, 1] = tangent.astype(sink.dtype)
    own_stats[h, 0:1, :] = top
    own_stats[h, 1:2, :] = total
    own_stats[h, 2:3, :] = mean_tan


def kernel(
    n_ctx,
    q_ref,
    k_ref,
    v_ref,
    qt_ref,
    kt_ref,
    vt_ref,
    tq_ref,
    tk_ref,
    cnt_ref,
    out_both,
    query,
    keyval,
    values_t,
    bias_own,
    bias_rows,
    bias,
    local,
    local_stats,
    sent,
    sent_stats,
    came,
    came_stats,
    outbuf,
    in_send,
    q_recv,
    kv_recv,
    zq_send,
    xq_send,
    fq_send,
    bias_send,
    bias_hop_send,
    bias_recv,
    part_send,
    part_recv,
    stat_send,
    stat_recv,
    out_send,
    out_recv,
    told,
    far_keyval,
    far_values_t,
    far_send,
    far_recv,
):
    out_p, out_t = out_both.at[0], out_both.at[1]
    ctx = lax.axis_index("ctx")
    uly = lax.axis_index("uly")
    core = lax.rem(uly, 2)
    yh = lax.rem(ctx, 2)
    base = ctx - yh
    y = yh * 2 + lax.div(uly, 2)
    other = uly + 1 - 2 * core
    ahead = lax.rem(ctx + 2, n_ctx)
    behind = lax.rem(ctx + n_ctx - 2, n_ctx)
    behind_or_here = lax.rem(ctx + (1 - core) * (n_ctx - 2), n_ctx)
    here_or_ahead = lax.rem(ctx + core * 2, n_ctx)
    at_home = core == yh

    barrier = pltpu.get_barrier_semaphore()
    chip = uly - core
    for step in range(4):
        place = lax.rem(y + step, 4)

        def greet():
            pl.semaphore_signal(
                barrier, inc=1, device_id=(base + lax.div(place, 2), lax.rem(place, 2) * 2), device_id_type=MESH
            )

        if step == 0:
            pl.when(core == 1)(greet)
        else:
            greet()
    for where in (ahead, behind):
        pl.semaphore_signal(barrier, inc=1, device_id=(where, chip + 1), device_id_type=MESH)

    lane = lax.broadcasted_iota(jnp.int32, (REACH * QT, MAXT), 1)
    code = lax.broadcasted_iota(jnp.int32, (REACH * QT, MAXT), 0)
    row = lax.broadcasted_iota(jnp.int32, (REACH * QT, 1), 0)
    usable = (lane < cnt_ref[0]) & (jnp.broadcast_to(tq_ref[...], code.shape) == uly)
    hit = usable & (jnp.broadcast_to(tk_ref[...], code.shape) == code)
    seen = jnp.max(jnp.where(hit, 1.0, 0.0), axis=1, keepdims=True)
    seen = jnp.maximum(seen, jnp.where(row == uly, 1.0, 0.0))
    bias_own[...] = jnp.broadcast_to((1.0 - seen) * NEG, (REACH * QT, HEAD))

    @pl.when(core == 0)
    def _():
        pl.semaphore_wait(barrier, 7)
        pl.semaphore_signal(told, inc=1, device_id=(ctx, other), device_id_type=MESH)

    @pl.when(core == 1)
    def _():
        pl.semaphore_wait(told, 1)

    own_rows = pl.ds(pl.multiple_of(uly * TILE, TILE), TILE)
    low_half, high_half = pl.ds(0, HEAD), pl.ds(HEAD, HEAD)

    def group_device(place):
        return (base + lax.div(place, 2), lax.rem(place, 2) * 2 + yh)

    def send_in(moves, first, j):
        for step in range(4):
            place = lax.rem(y + step, 4)
            cols = pl.ds(pl.multiple_of((place * LOCAL_HEADS + j) * HEAD, HEAD), HEAD)

            def remote():
                for a, (src, dst, sem) in enumerate(moves):
                    pltpu.make_async_remote_copy(
                        src_ref=src.at[:, cols],
                        dst_ref=dst,
                        send_sem=in_send.at[step, first + a],
                        recv_sem=sem,
                        device_id=group_device(place),
                        device_id_type=MESH,
                    ).start()

            def stay():
                for src, dst, sem in moves:
                    pltpu.make_async_copy(src.at[:, cols], dst, sem).start()

            if step == 0:
                pl.when(at_home)(stay)
                pl.when(jnp.logical_not(at_home))(remote)
            else:
                remote()

    def send_q(j):
        send_in(
            (
                (q_ref, query.at[j, 0, own_rows, high_half], q_recv.at[j, 0]),
                (qt_ref, query.at[j, 0, own_rows, low_half], q_recv.at[j, 0]),
            ),
            0,
            j,
        )

    def send_kv(j):
        send_in(
            (
                (k_ref, keyval.at[j, 0, own_rows, low_half], kv_recv.at[j]),
                (kt_ref, keyval.at[j, 0, own_rows, high_half], kv_recv.at[j]),
                (v_ref, keyval.at[j, 1, own_rows, low_half], kv_recv.at[j]),
                (vt_ref, keyval.at[j, 1, own_rows, high_half], kv_recv.at[j]),
            ),
            2,
            j,
        )

    def bias_copy(step):
        return pltpu.make_async_remote_copy(
            src_ref=bias_own,
            dst_ref=bias_rows.at[0, uly],
            send_sem=bias_send.at[step],
            recv_sem=bias_recv.at[0],
            device_id=group_device(lax.rem(y + step, 4)),
            device_id_type=MESH,
        )

    def hop(j, src, dst, sems, ctx_to, uly_to):
        return pltpu.make_async_remote_copy(
            src_ref=query.at[j, src],
            dst_ref=query.at[j, dst],
            send_sem=sems.at[j],
            recv_sem=q_recv.at[j, dst],
            device_id=(ctx_to, uly_to),
            device_id_type=MESH,
        )

    def bias_hop(src, dst, way, ctx_to, uly_to):
        return pltpu.make_async_remote_copy(
            src_ref=bias_rows.at[src],
            dst_ref=bias_rows.at[dst],
            send_sem=bias_hop_send.at[way],
            recv_sem=bias_recv.at[dst],
            device_id=(ctx_to, uly_to),
            device_id_type=MESH,
        )

    def wait_query(j, slot):
        pltpu.make_async_copy(query.at[j, slot], query.at[j, slot], q_recv.at[j, slot]).wait()

    def wait_bias(slot):
        pltpu.make_async_copy(bias_rows.at[slot], bias_rows.at[slot], bias_recv.at[slot]).wait()

    def spread_bias(slot, back, to):
        for t in range(QT):
            for c in range(QT):
                at = back * QT + c
                bias[to, t, c] = jnp.broadcast_to(bias_rows[slot, t, at : at + 1, :], (8, HEAD))

    def forward_own(j):
        wait_query(j, 0)
        hop(j, 0, 2, zq_send, behind, uly).start()

        @pl.when(core == 1)
        def _():
            hop(j, 0, 1, xq_send, ctx, other).start()

        @pl.when(j == 0)
        def _():
            wait_bias(0)
            bias_hop(0, 2, 0, behind, uly).start()

            @pl.when(core == 1)
            def _():
                bias_hop(0, 1, 1, ctx, other).start()

            spread_bias(0, 0, 0)

    def forward_next(j):
        wait_query(j, 2)

        @pl.when((core == 1) | far_by_query(j))
        def _():
            hop(j, 2, 3, fq_send, behind_or_here, other).start()

        @pl.when(core == 0)
        def _():
            hop(j, 2, 1, xq_send, ctx, other).start()

        @pl.when(j == 0)
        def _():
            wait_bias(2)
            bias_hop(2, 3, 2, behind_or_here, other).start()

            @pl.when(core == 0)
            def _():
                bias_hop(2, 1, 1, ctx, other).start()

            spread_bias(2, 2, 2)
            spread_bias(2, 3, REACH)

    def part_copies(h, j, src, dst, ctx_to, uly_to):
        return [
            pltpu.make_async_remote_copy(
                src_ref=a.at[j, src, h],
                dst_ref=b.at[j, dst, h],
                send_sem=ss.at[j, src, h],
                recv_sem=rs.at[j, dst, h],
                device_id=(ctx_to, uly_to),
                device_id_type=MESH,
            )
            for a, b, ss, rs in (
                (sent, came, part_send, part_recv),
                (sent_stats, came_stats, stat_send, stat_recv),
            )
        ]

    def start_part(*args):
        for copy in part_copies(*args):
            copy.start()

    def wait_part(h, j, dst):
        for ref, sem in ((came, part_recv), (came_stats, stat_recv)):
            pltpu.make_async_copy(ref.at[j, dst, h], ref.at[j, dst, h], sem.at[j, dst, h]).wait()

    def work(j, slot, *way):
        kept = slot % 2 == 0
        place = (j, slot // 2)
        sink, stats = (local, local_stats) if kept else (sent, sent_stats)
        for h in range(HALVES):
            attend(
                h,
                query.at[j, slot],
                keyval.at[j, 0],
                values_t.at[j],
                bias.at[slot],
                sink.at[place],
                stats.at[place],
            )
            if not kept:
                start_part(h, j, slot // 2, *way)

    def absorb(h, j, which, dst, sink):
        merge(h, local.at[j, which], local_stats.at[j, which], came.at[j, dst], came_stats.at[j, dst], sink)

    def send_out(h, j):
        cols = pl.ds(pl.multiple_of((y * LOCAL_HEADS + j) * HEAD, HEAD), HEAD)
        for t in range(h * PART // TILE, (h + 1) * PART // TILE):
            def remote():
                for a, out in enumerate((out_p, out_t)):
                    pltpu.make_async_remote_copy(
                        src_ref=outbuf.at[j, a, pl.ds(t * TILE, TILE), :],
                        dst_ref=out.at[:, cols],
                        send_sem=out_send.at[t, a],
                        recv_sem=out_recv.at[a],
                        device_id=(base + core, t),
                        device_id_type=MESH,
                    ).start()

            def stay():
                for a, out in enumerate((out_p, out_t)):
                    pltpu.make_async_copy(
                        outbuf.at[j, a, pl.ds(t * TILE, TILE), :], out.at[:, cols], out_recv.at[a]
                    ).start()

            here = at_home & (uly == t)
            pl.when(here)(stay)
            pl.when(jnp.logical_not(here))(remote)

    @pl.when(at_home)
    def _():
        pltpu.make_async_copy(bias_own, bias_rows.at[0, uly], bias_recv.at[0]).start()

    @pl.when(jnp.logical_not(at_home))
    def _():
        bias_copy(0).start()

    for step in range(1, 4):
        bias_copy(step).start()
    def far_by_query(j):
        return look_up(MEET, j) == 0

    def keys_ahead(j):
        return pltpu.make_async_remote_copy(
            src_ref=keyval.at[j],
            dst_ref=far_keyval.at[j],
            send_sem=far_send.at[j],
            recv_sem=far_recv.at[j],
            device_id=(ahead, other),
            device_id_type=MESH,
        )

    def take_kv(j):
        pltpu.make_async_copy(keyval.at[j], keyval.at[j], kv_recv.at[j]).wait()
        values_t[j] = keyval[j, 1].T

    def work_far(j):
        pltpu.make_async_copy(far_keyval.at[j], far_keyval.at[j], far_recv.at[j]).wait()
        far_values_t[...] = far_keyval[j, 1].T
        for h in range(HALVES):
            attend(
                h,
                query.at[j, 2],
                far_keyval.at[j, 0],
                far_values_t,
                bias.at[REACH],
                came.at[j, 1],
                came_stats.at[j, 1],
            )

    def work_from(j, slot, first, *way):
        wait_query(j, slot)

        @pl.when(j == first)
        def _():
            wait_bias(slot)
            spread_bias(slot, slot, slot)

        work(j, slot, *way)

    @pl.loop(0, 2 * LOCAL_HEADS)
    def _(at):
        item = jnp.where(yh == 0, look_up(SEND_EVEN, at), look_up(SEND_ODD, at))
        j = item % 8
        pl.when(item < 8)(lambda: send_q(j))
        pl.when(item >= 8)(lambda: send_kv(j))

    @pl.when(core == 1)
    def _():
        pl.semaphore_wait(barrier, 4)
        pl.semaphore_signal(told, inc=1, device_id=(ctx, other), device_id_type=MESH)

    @pl.when(core == 0)
    def _():
        pl.semaphore_wait(told, 1)

    @pl.loop(0, len(PLAN_EVEN))
    def _(at):
        item = jnp.where(core == 0, look_up(PLAN_EVEN, at), look_up(PLAN_ODD, at))
        j, what = item % 8, item // 8

        def attend_pass_previous():
            work_from(j, 1, jnp.where(core == 0, 0, 0), 1 - core, ctx, other)

        def attend_pass_far():
            @pl.when((core == 0) | far_by_query(j))
            def _():
                work_from(j, 3, jnp.where(core == 0, 0, 4), core, here_or_ahead, other)

            @pl.when((core == 1) & jnp.logical_not(far_by_query(j)))
            def _():
                keys_ahead(j).start()

        def pass_on():
            for h in range(HALVES):
                @pl.when((core == 0) & far_by_query(j))
                def _():
                    wait_part(h, j, 1)

                @pl.when(core == 0)
                def _():
                    absorb(h, j, 1, 1, local.at[j, 1])

                wait_part(h, j, 0)
                absorb(h, j, 1, 0, sent.at[j, 2])
                sent_stats[j, 2, h] = local_stats[j, 1, h]
                start_part(h, j, 2, 2, ahead, uly)

        def finish():
            @pl.when(core == 1)
            def _():
                for h in range(HALVES):
                    wait_part(h, j, 1)
                    absorb(h, j, 0, 1, local.at[j, 0])

            for h in range(HALVES):
                wait_part(h, j, 2)
                absorb(h, j, 0, 2, local.at[j, 0])
                rows = pl.ds(h * PART, PART)
                outbuf[j, 0, rows, :] = local[j, 0, h, 0].T.astype(jnp.bfloat16)
                outbuf[j, 1, rows, :] = local[j, 0, h, 1].T.astype(jnp.bfloat16)
                send_out(h, j)

        steps = (
            lambda: forward_own(j),
            lambda: forward_next(j),
            lambda: take_kv(j),
            lambda: work(j, 0),
            attend_pass_previous,
            lambda: work(j, 2),
            attend_pass_far,
            pass_on,
            finish,
            lambda: work_far(j),
        )
        for number, step in enumerate(steps):
            pl.when(what == number)(step)

    group = pl.ds(0, LOCAL_HEADS * HEAD)
    for step in range(4):
        def gone():
            for a, src in enumerate((q_ref, qt_ref, k_ref, kt_ref, v_ref, vt_ref)):
                pltpu.make_async_copy(src.at[:, group], src.at[:, group], in_send.at[step, a]).wait()
            bias_copy(step).wait_send()

        if step == 0:
            pl.when(jnp.logical_not(at_home))(gone)
        else:
            gone()

    bias_hop(0, 2, 0, behind, uly).wait_send()
    bias_hop(0, 1, 1, ctx, other).wait_send()
    bias_hop(2, 3, 2, behind_or_here, other).wait_send()

    @pl.loop(0, LOCAL_HEADS)
    def _(j):
        hop(j, 0, 2, zq_send, behind, uly).wait_send()
        hop(j, 0, 1, xq_send, ctx, other).wait_send()

        @pl.when((core == 1) | far_by_query(j))
        def _():
            hop(j, 2, 3, fq_send, behind_or_here, other).wait_send()

        @pl.when((core == 0) | far_by_query(j))
        def _():
            for h in range(HALVES):
                for copy in part_copies(h, j, 1, core, here_or_ahead, other):
                    copy.wait_send()

        @pl.when((core == 1) & jnp.logical_not(far_by_query(j)))
        def _():
            keys_ahead(j).wait_send()

        for h in range(HALVES):
            for copy in part_copies(h, j, 0, 1 - core, ctx, other) + part_copies(h, j, 2, 2, ahead, uly):
                copy.wait_send()

    for t in range(QT):
        @pl.when(jnp.logical_not(at_home & (uly == t)))
        def _():
            for a, out in enumerate((out_p, out_t)):
                pltpu.make_async_copy(out.at[:, group], out.at[:, group], out_send.at[t, a]).wait()

    pltpu.make_async_copy(out_p, out_p, out_recv.at[0]).wait()
    pltpu.make_async_copy(out_t, out_t, out_recv.at[1]).wait()


def on_device(n_ctx, query_rows, key_rows, value_rows, query_tan, key_tan, value_tan, tile_query, tile_key, tile_count):
    heads = LOCAL_HEADS
    anyspace = pl.BlockSpec(memory_space=pl.ANY)
    hbm = pl.BlockSpec(memory_space=pltpu.HBM)
    vmem = pl.BlockSpec(memory_space=pltpu.VMEM)
    dma = pltpu.SemaphoreType.DMA
    both = pl.pallas_call(
        functools.partial(kernel, n_ctx),
        out_shape=jax.ShapeDtypeStruct((2,) + query_rows.shape, jnp.bfloat16),
        in_specs=[hbm] * 6 + [vmem, vmem, pl.BlockSpec(memory_space=pltpu.SMEM)],
        out_specs=anyspace,
        scratch_shapes=[
            pltpu.VMEM((heads, REACH, CT, 2 * HEAD), jnp.bfloat16),
            pltpu.VMEM((heads, 2, CT, 2 * HEAD), jnp.bfloat16),
            pltpu.VMEM((heads, 2 * HEAD, CT), jnp.bfloat16),
            pltpu.VMEM((REACH * QT, HEAD), jnp.float32),
            pltpu.VMEM((REACH, QT, REACH * QT, HEAD), jnp.float32),
            pltpu.VMEM((REACH + 1, QT, QT, 8, HEAD), jnp.float32),
            pltpu.VMEM((heads, 2, HALVES, 2, HEAD, PART), jnp.float32),
            pltpu.VMEM((heads, 2, HALVES, 8, PART), jnp.float32),
            pltpu.VMEM((heads, 3, HALVES, 2, HEAD, PART), jnp.bfloat16),
            pltpu.VMEM((heads, 3, HALVES, 8, PART), jnp.float32),
            pltpu.VMEM((heads, 3, HALVES, 2, HEAD, PART), jnp.bfloat16),
            pltpu.VMEM((heads, 3, HALVES, 8, PART), jnp.float32),
            pltpu.VMEM((heads, 2, CT, HEAD), jnp.bfloat16),
            dma((4, 6)),
            dma((heads, REACH)),
            dma((heads,)),
            dma((heads,)),
            dma((heads,)),
            dma((heads,)),
            dma((4,)),
            dma((3,)),
            dma((REACH,)),
            dma((heads, 3, HALVES)),
            dma((heads, 3, HALVES)),
            dma((heads, 3, HALVES)),
            dma((heads, 3, HALVES)),
            dma((QT, 2)),
            dma((2,)),
            pltpu.SemaphoreType.REGULAR,
            pltpu.VMEM((heads, 2, CT, 2 * HEAD), jnp.bfloat16),
            pltpu.VMEM((2 * HEAD, CT), jnp.bfloat16),
            dma((heads,)),
            dma((heads,)),
        ],
        compiler_params=pltpu.CompilerParams(
            collective_id=0, has_side_effects=True, vmem_limit_bytes=60 * 1024 * 1024
        ),
        cost_estimate=pl.CostEstimate(
            flops=heads * CT * CT * REACH * HEAD * 12,
            bytes_accessed=12 * TILE * 2560,
            transcendentals=heads * CT * CT * REACH,
        ),
        name="band_attention",
    )(query_rows, key_rows, value_rows, query_tan, key_tan, value_tan, tile_query, tile_key, tile_count)
    return both[0], both[1]


def solution(mesh):
    rows = P(("ctx", "uly"), None)
    return jax.shard_map(
        functools.partial(on_device, mesh.shape["ctx"]),
        mesh=mesh,
        in_specs=(rows,) * 6 + (P("ctx", None), P("ctx", None), P("ctx")),
        out_specs=(rows, rows),
        check_vma=False,
    )
```
